32 devices in a mesh: mid: 4 (over y, core), leaf: 8 (over z, x).
Axes of the slice: x: 2, y: 2, z: 4, core: 2. Of those that a mesh axis runs over, the one named last changes fastest.
Arguments:
- queries: bfloat16 [8192, 4096], P(('mid', 'leaf')), may hold values from -128 to 128
- out_grad: bfloat16 [8192, 4096], P(('mid', 'leaf')), may hold values from -6 to 6
- leaf_keys: bfloat16 [8192, 1024], P(('mid', 'leaf')), may hold values from -6 to 6
- leaf_values: bfloat16 [8192, 1024], P(('mid', 'leaf')), may hold values from -6 to 6
- mid_keys: bfloat16 [512, 1024], P(('mid', 'leaf')), may hold values from -6 to 6
- mid_values: bfloat16 [512, 1024], P(('mid', 'leaf')), may hold values from -6 to 6
- root_keys: bfloat16 [64, 1024], P(('mid', 'leaf')), may hold values from -4 to 4
- root_values: bfloat16 [64, 1024], P(('mid', 'leaf')), may hold values from -6 to 6
- mid_len: int32 [4], P('mid'), may hold values from 1 to 128, 384 in all
- leaf_len: int32 [32], P(('mid', 'leaf')), may hold values from 1 to 256, 5120 in all
Outputs:
- query_grad: bfloat16 [8192, 4096], P(('mid', 'leaf'))
- leaf_key_grad: bfloat16 [8192, 1024], P(('mid', 'leaf'))
- leaf_value_grad: bfloat16 [8192, 1024], P(('mid', 'leaf'))
- mid_key_grad: float32 [512, 1024], P(('mid', 'leaf'))
- mid_value_grad: float32 [512, 1024], P(('mid', 'leaf'))
- root_key_grad: float32 [64, 1024], P(('mid', 'leaf'))
- root_value_grad: float32 [64, 1024], P(('mid', 'leaf'))
The draws below stay inside these ranges and needn't reach their ends.
Inputs may be any that keep to these rules, and one draw needn't show every extreme that they name: `mid_len`: at least one mid branch has all 128 tokens live. `leaf_len`: at least one leaf has all 256 tokens live.
All inputs are finite; a program needn't handle non-finite values. No bound on the sum of `mid_len` or of `leaf_len` on one device may be relied on, other than what follows from the above.
Results may differ from the reference program's by a relative error of at most 0.013.
Values may be sent and summed in bfloat16 or wider, within the bound.
No kernel may reach another device: no remote copies, remote signals or barrier semaphores. Data moves between devices by JAX's collectives and lax.ppermute only.
A program may use at most 128 MiB of HBM per device.

```python
import math
import jax
import jax.numpy as jnp
import numpy as np
from jax import lax

QH = 32
KVH = 8
HD = 128
LEAF = 256
BRANCHES = 4
BRANCH_LEAVES = 8
LEAVES = 32
MID = 128
ROOT = 64


def shared_root(key):
    return jnp.clip(jax.random.normal(jax.random.fold_in(key, 101), (ROOT, KVH * HD), jnp.float32), -4.0, 4.0)


def draw_root_keys(key, part):
    base_keys = shared_root(key)
    return base_keys.astype(jnp.bfloat16)


def draw_queries(key, part):
    key = jax.random.fold_in(key, 7)
    total_rows = LEAVES * LEAF
    drawn = jnp.clip(jax.random.normal(jax.random.fold_in(key, 1), (total_rows, QH * HD), jnp.float32), -4.0, 4.0)
    return drawn.astype(jnp.bfloat16)


def levels(stream_key, extent, split, smallest, largest):
    factor_of, own = 1.0, jax.random.fold_in(stream_key, 6)
    for axis_at, shards_of in split:
        steps = jnp.exp(jax.random.uniform(jax.random.fold_in(own, axis_at), (shards_of,), jnp.float32, smallest / len(split), largest / len(split)))
        factor_of = factor_of * jnp.repeat(steps, extent[axis_at] // shards_of).reshape([-1 if axis == axis_at else 1 for axis in range(len(extent))])
    return factor_of


def profile(amount, total, reach, skew):
    portions = [(1 << 20) // math.isqrt(grade ** skew) + 1 for grade in range(2, amount + 1)]
    surplus, holding = total - reach - (amount - 1), [1] * (amount - 1)
    while surplus > 0:
        candidates = [i for i in range(amount - 1) if holding[i] < reach]
        pool, remaining = sum([portions[i] for i in candidates]), surplus
        for i in candidates:
            addition = min(reach - holding[i], max(1, remaining * portions[i] // pool), surplus)
            holding[i] = holding[i] + addition
            surplus = surplus - addition
    return np.array([reach] + holding)


def ragged_sizes(own_key, number_of, total, reach, lean):
    if number_of == 2:
        one = jax.random.randint(own_key, (), max(1, total - reach), min(reach, total - 1) + 1)
        return jnp.stack([one, total - one])
    tallies = jnp.asarray(profile(number_of, total, reach, lean), jnp.int32)
    twos = (number_of - 1) // 2
    source_of, taker = tallies[1:1 + 2 * twos:2], tallies[2:2 + 2 * twos:2]
    room = jnp.minimum(source_of - 1, reach - taker)
    shifted = jax.random.randint(jax.random.fold_in(own_key, 1), (twos,), 0, 1 << 20) % (room + 1)
    tallies = tallies.at[1:1 + 2 * twos:2].set(source_of - shifted).at[2:2 + 2 * twos:2].set(taker + shifted)
    return tallies[jax.random.permutation(jax.random.fold_in(own_key, 2), number_of)]


def normal_values(stream_key, shape, deviation, most, cuts=(), kind=jnp.bfloat16):
    gain = levels(stream_key, shape, cuts, -0.22, 0.18) if cuts else 1.0
    values = jax.random.normal(stream_key, shape, jnp.float32) * deviation * gain
    return jnp.minimum(jnp.maximum(values, -most), most).astype(kind)


def setup_inputs(seed: int = 0) -> dict:
    arg_keys = jax.random.split(jax.random.key(seed), 11)
    queries = draw_queries(jax.random.fold_in(arg_keys[10], 71), 0)
    out_grad = normal_values(arg_keys[1], (LEAVES * LEAF, QH * HD), 1.0, 6.0, ((0, 32),))
    leaf_keys = normal_values(arg_keys[2], (LEAVES * LEAF, KVH * HD), 1.0, 6.0, ((0, 32),))
    leaf_values = normal_values(arg_keys[3], (LEAVES * LEAF, KVH * HD), 1.0, 6.0, ((0, 32),))
    mid_keys = normal_values(arg_keys[4], (BRANCHES * MID, KVH * HD), 1.0, 6.0, ((0, 32),))
    mid_values = normal_values(arg_keys[5], (BRANCHES * MID, KVH * HD), 1.0, 6.0, ((0, 32),))
    root_keys = draw_root_keys(jax.random.fold_in(arg_keys[10], 71), 0)
    root_values = normal_values(arg_keys[7], (ROOT, KVH * HD), 1.0, 6.0, ((0, 32),))
    mid_len = ragged_sizes(arg_keys[8], BRANCHES, BRANCHES * MID * 3 // 4, MID, 1).astype(jnp.int32)
    leaf_len = ragged_sizes(arg_keys[9], LEAVES, LEAVES * LEAF * 5 // 8, LEAF, 1).astype(jnp.int32)
    return {"queries": queries, "out_grad": out_grad, "leaf_keys": leaf_keys, "leaf_values": leaf_values, "mid_keys": mid_keys, "mid_values": mid_values, "root_keys": root_keys, "root_values": root_values, "mid_len": mid_len, "leaf_len": leaf_len}


def leaf_backward(queries, out_grad, all_keys, all_values, root_rows, mid_rows, mid_live, leaf_live):
    leaf_rows = queries.shape[0]
    key_rows = all_keys.shape[0]
    heads_per = QH // KVH
    span_cols = heads_per * HD
    column = jnp.arange(key_rows, dtype=jnp.int32)[None, :]
    row_ids = jnp.arange(leaf_rows, dtype=jnp.int32)[:, None]
    offset = root_rows + mid_rows
    leaf_pos = column - offset
    in_root = column < root_rows
    in_mid = (column >= root_rows) & (column < offset) & (column - root_rows < mid_live)
    in_leaf = (leaf_pos >= 0) & (leaf_pos <= row_ids) & (leaf_pos < leaf_live)
    allowed = in_root | in_mid | in_leaf
    live_rows = (jnp.arange(leaf_rows, dtype=jnp.int32) < leaf_live).astype(jnp.float32)[None, :, None]
    factor = HD ** -0.5
    query_wide = queries.astype(jnp.float32)
    grad_wide = out_grad.astype(jnp.float32)
    keys_wide = all_keys.astype(jnp.float32)
    values_wide = all_values.astype(jnp.float32)

    def one_head(head_index, buffers):
        query_acc, key_acc, value_acc = buffers
        query_part = lax.dynamic_slice_in_dim(query_wide, head_index * span_cols, span_cols, 1).reshape(leaf_rows, heads_per, HD)
        grad_part = lax.dynamic_slice_in_dim(grad_wide, head_index * span_cols, span_cols, 1).reshape(leaf_rows, heads_per, HD)
        key_part = lax.dynamic_slice_in_dim(keys_wide, head_index * HD, HD, 1)
        value_part = lax.dynamic_slice_in_dim(values_wide, head_index * HD, HD, 1)
        scores = factor * jnp.einsum("igd,jd->gij", query_part, key_part)
        scores = jnp.where(allowed[None], scores, -1e30)
        row_max = jnp.max(scores, axis=-1, keepdims=True)
        weights = jnp.exp(scores - row_max)
        probs = weights / jnp.sum(weights, axis=-1, keepdims=True) * live_rows
        probs_low = lax.optimization_barrier(probs.astype(jnp.bfloat16)).astype(jnp.float32)
        value_term = jnp.einsum("gij,igd->jd", probs_low, grad_part)
        dprobs = jnp.einsum("igd,jd->gij", grad_part, value_part)
        row_dots = jnp.sum(probs * dprobs, axis=-1, keepdims=True)
        dscores = lax.optimization_barrier((probs * (dprobs - row_dots)).astype(jnp.bfloat16)).astype(jnp.float32)
        query_term = factor * jnp.einsum("gij,jd->igd", dscores, key_part)
        key_term = factor * jnp.einsum("gij,igd->jd", dscores, query_part)
        query_acc = lax.dynamic_update_slice_in_dim(query_acc, query_term.reshape(leaf_rows, span_cols).astype(jnp.bfloat16), head_index * span_cols, 1)
        key_acc = lax.dynamic_update_slice_in_dim(key_acc, key_term, head_index * HD, 1)
        value_acc = lax.dynamic_update_slice_in_dim(value_acc, value_term, head_index * HD, 1)
        return query_acc, key_acc, value_acc

    start = (jnp.zeros((leaf_rows, QH * HD), jnp.bfloat16), jnp.zeros((key_rows, KVH * HD), jnp.float32), jnp.zeros((key_rows, KVH * HD), jnp.float32))
    return lax.fori_loop(0, KVH, one_head, start)


def reference(queries, out_grad, leaf_keys, leaf_values, mid_keys, mid_values, root_keys, root_values, mid_len, leaf_len):
    kv_cols = KVH * HD
    query_cols = QH * HD
    by_leaf = (queries.reshape(BRANCHES, BRANCH_LEAVES, LEAF, query_cols), out_grad.reshape(BRANCHES, BRANCH_LEAVES, LEAF, query_cols), leaf_keys.reshape(BRANCHES, BRANCH_LEAVES, LEAF, kv_cols), leaf_values.reshape(BRANCHES, BRANCH_LEAVES, LEAF, kv_cols), leaf_len.reshape(BRANCHES, BRANCH_LEAVES))
    by_branch = (mid_keys.reshape(BRANCHES, MID, kv_cols), mid_values.reshape(BRANCHES, MID, kv_cols), mid_len)

    def branch_step(root_totals, items):
        leaf_items = items[:5]
        branch_keys, branch_values, branch_live = items[5], items[6], items[7]

        def leaf_step(totals, piece):
            query_part, grad_part, own_keys, own_values, own_live = piece
            all_keys = jnp.concatenate([root_keys, branch_keys, own_keys], 0)
            all_values = jnp.concatenate([root_values, branch_values, own_values], 0)
            query_out, key_terms, value_terms = leaf_backward(query_part, grad_part, all_keys, all_values, ROOT, MID, branch_live, own_live)
            totals = (totals[0] + key_terms[ROOT:ROOT + MID], totals[1] + value_terms[ROOT:ROOT + MID], totals[2] + key_terms[:ROOT], totals[3] + value_terms[:ROOT])
            return totals, (query_out, key_terms[ROOT + MID:].astype(jnp.bfloat16), value_terms[ROOT + MID:].astype(jnp.bfloat16))

        start = (jnp.zeros((MID, kv_cols), jnp.float32), jnp.zeros((MID, kv_cols), jnp.float32), jnp.zeros((ROOT, kv_cols), jnp.float32), jnp.zeros((ROOT, kv_cols), jnp.float32))
        totals, leaf_outs = lax.scan(leaf_step, start, leaf_items)
        root_totals = (root_totals[0] + totals[2], root_totals[1] + totals[3])
        return root_totals, (leaf_outs[0], leaf_outs[1], leaf_outs[2], totals[0], totals[1])

    start_root = (jnp.zeros((ROOT, kv_cols), jnp.float32), jnp.zeros((ROOT, kv_cols), jnp.float32))
    root_totals, stacked = lax.scan(branch_step, start_root, by_leaf + by_branch)
    query_grad = stacked[0].reshape(LEAVES * LEAF, query_cols)
    leaf_key_grad = stacked[1].reshape(LEAVES * LEAF, kv_cols)
    leaf_value_grad = stacked[2].reshape(LEAVES * LEAF, kv_cols)
    mid_key_grad = stacked[3].reshape(BRANCHES * MID, kv_cols)
    mid_value_grad = stacked[4].reshape(BRANCHES * MID, kv_cols)
    return (query_grad, leaf_key_grad, leaf_value_grad, mid_key_grad, mid_value_grad, root_totals[0], root_totals[1])
```

```python
import functools
import math

import jax
import jax.numpy as jnp
from jax import lax
from jax.experimental import pallas as pl
from jax.experimental.pallas import tpu as pltpu
from jax.sharding import PartitionSpec as P

HD = 128
FACTOR = HD**-0.5
LOG2E = math.log2(math.e)
CHUNK = 16
NEG = -1e30
NT = (((1,), (1,)), ((), ()))
NN = (((1,), (0,)), ((), ()))
TN = (((0,), (0,)), ((), ()))


def dot(a, b, dims):
    return lax.dot_general(a, b, dims, preferred_element_type=jnp.float32)


def stacked(ref, part, half, heads_per):
    rows = slice(part * half, (part + 1) * half)
    return jnp.concatenate([ref[rows, h * HD : (h + 1) * HD] for h in range(heads_per)], 0)


def fold(x):
    return [x[i : i + 8] for i in range(0, x.shape[0], 8)]


def total_of(so_far, x, op):
    for y in fold(x):
        so_far = y if so_far is None else op(so_far, y)
    return so_far


def own_kernel(
    parity, _, q_hbm, g_hbm, k_hbm, v_hbm, q_ref, g_ref, k_ref, v_ref, e_ref, dp_ref, stats_ref, sems
):
    count, leaf_rows, span = q_ref.shape
    half = leaf_rows // 2
    heads_per = span // HD
    lanes = heads_per * half

    def copies(i):
        h = 2 * i + parity
        wide = pl.ds(pl.multiple_of(h * span, span), span)
        at = pl.ds(pl.multiple_of(h * HD, HD), HD)
        pairs = [
            (q_hbm.at[:, wide], q_ref.at[i]),
            (g_hbm.at[:, wide], g_ref.at[i]),
            (k_hbm.at[:, at], k_ref.at[i]),
            (v_hbm.at[:, at], v_ref.at[i]),
        ]
        return [pltpu.make_async_copy(x, y, sems.at[i, j]) for j, (x, y) in enumerate(pairs)]

    for i in range(count):
        for c in copies(i):
            c.start()
    chunk_row = lax.broadcasted_iota(jnp.int32, (CHUNK, half), 0)
    chunk_col = lax.broadcasted_iota(jnp.int32, (CHUNK, half), 1)

    @pl.loop(0, count)
    def one_head(i):
        for c in copies(i):
            c.wait()

        def scores(part):
            n, at = (part + 1) * half, part * half
            e_ref[i, at : at + n] = dot(k_ref[i, :n], stacked(q_ref.at[i], part, half, heads_per), NT)
            dp_ref[i, at : at + n] = dot(v_ref[i, :n], stacked(g_ref.at[i], part, half, heads_per), NT)

        def softmax(part):
            n, at = (part + 1) * half, part * half
            cols = slice(part * lanes, (part + 1) * lanes)

            def masked_chunk(r):
                s = e_ref[i, at + r : at + r + CHUNK]
                if r < n - half:
                    return s
                mask = chunk_row + (r - n + half) <= chunk_col
                return jnp.concatenate(
                    [jnp.where(mask, s[:, g * half : (g + 1) * half], NEG) for g in range(heads_per)], 1
                )

            starts = range(0, n, CHUNK)
            top = total = rd = None
            for r in starts:
                top = total_of(top, masked_chunk(r), jnp.maximum)
            top = jnp.max(top, axis=0, keepdims=True)
            for r in starts:
                e = jnp.exp2((masked_chunk(r) - top) * (FACTOR * LOG2E))
                e_ref[i, at + r : at + r + CHUNK] = e
                total = total_of(total, e, jnp.add)
                rd = total_of(rd, e * dp_ref[i, at + r : at + r + CHUNK], jnp.add)
            stats_ref[i, 0:1, cols] = top
            stats_ref[i, 1:2, cols] = jnp.sum(total, axis=0, keepdims=True)
            stats_ref[i, 2:3, cols] = jnp.sum(rd, axis=0, keepdims=True)

        scores(0)
        scores(1)
        softmax(0)
        softmax(1)


def places(slots):
    if slots < 4:
        return [(s, 0) for s in range(slots)]
    return [(0, 0), (1, 0), (2, 0), (2, 1)] + [(s - 1, 0) for s in range(4, slots)]


def terms_kernel(slots, mid_part, where_ref, mid_len_ref, leaf_len_ref, *refs):
    own_parts = refs[:7], refs[7:14]
    arrays = places(slots)[-1][0] + 1
    block_refs = [refs[14 + i].at[pl.ds(j * 2 * mid_part, 2 * mid_part)] for i, j in places(slots)]
    root_refs = refs[14 + arrays : 16 + arrays]
    outs = refs[16 + arrays :]
    keys_ref, ds_ref, dk_ref, dv_ref = outs[:4]
    dmid_refs = outs[4 : 4 + slots]
    droot_refs = outs[4 + slots : 6 + slots]
    s_refs, dp_refs, p_refs = (outs[6 + slots + 2 * i : 8 + slots + 2 * i] for i in range(3))
    root_half = root_refs[0].shape[0] // 2
    me = where_ref[0]
    mid_live = mid_len_ref[0]
    leaf_live = leaf_len_ref[0]
    pairs, leaf_rows, span = own_parts[0][0].shape
    half = leaf_rows // 2
    heads_per = span // HD
    mid_rows = slots * mid_part
    root_rows = 2 * root_half
    shared = root_rows + mid_rows
    lanes = heads_per * half
    sizes = [shared + half, shared + 2 * half]
    chunk_row = lax.broadcasted_iota(jnp.int32, (CHUNK, half), 0)
    lane = lax.broadcasted_iota(jnp.int32, (1, half), 1)

    def live(part, x):
        alive = lane + part * half < leaf_live
        return jnp.concatenate(
            [jnp.where(alive, x[:, g * half : (g + 1) * half], 0.0) for g in range(heads_per)], 1
        )

    def masked_chunk(s_ref, r):
        s = s_ref[r : r + CHUNK]
        if r < root_rows:
            return s
        slot, rest = divmod(r - root_rows, mid_part)
        mask = chunk_row < mid_live - rest - jnp.bitwise_xor(me, slot) * mid_part
        return jnp.concatenate(
            [jnp.where(mask, s[:, g * half : (g + 1) * half], NEG) for g in range(heads_per)], 1
        )

    class Head:
        def __init__(self, i, parity):
            self.i = i
            self.h = h = 2 * i + parity
            self.at = pl.ds(pl.multiple_of(h * HD, HD), HD)
            q_ref, g_ref, k_ref, _, self.e_ref, self.own_dp_ref, self.stats_ref = own_parts[parity]
            self.keys = self.whole(0)
            self.values = self.whole(1)
            keys_ref[h, :shared] = self.keys
            keys_ref[h, shared:] = k_ref[i]
            self.qs = [stacked(q_ref.at[i], p, half, heads_per) for p in range(2)]
            self.gs = [stacked(g_ref.at[i], p, half, heads_per) for p in range(2)]
            self.dk, self.dv = [None, None], [None, None]

        def whole(self, which):
            at = self.at
            roots = [r[which * root_half : (which + 1) * root_half, at] for r in root_refs]
            mids = [r[which * mid_part : (which + 1) * mid_part, at] for r in block_refs]
            return jnp.concatenate(roots + mids, 0)

        def scores(self, part):
            s_refs[part][...] = dot(self.keys, self.qs[part], NT)
            dp_refs[part][...] = dot(self.values, self.gs[part], NT)

        def softmax(self, part):
            s_ref, dp_ref, p_ref = s_refs[part], dp_refs[part], p_refs[part]
            cols = slice(part * lanes, (part + 1) * lanes)
            own_top = self.stats_ref[self.i, 0:1, cols]
            top = total = rd = None
            starts = range(0, shared, CHUNK)
            for r in starts:
                top = total_of(top, masked_chunk(s_ref, r), jnp.maximum)
            top = jnp.maximum(jnp.max(top, axis=0, keepdims=True), own_top)
            own = jnp.exp2((own_top - top) * (FACTOR * LOG2E))
            for r in starts:
                e = jnp.exp2((masked_chunk(s_ref, r) - top) * (FACTOR * LOG2E))
                s_ref[r : r + CHUNK] = e
                total = total_of(total, e, jnp.add)
                rd = total_of(rd, e * dp_ref[r : r + CHUNK], jnp.add)
            total = jnp.sum(total, axis=0, keepdims=True) + own * self.stats_ref[self.i, 1:2, cols]
            inv = live(part, 1.0 / total)
            rd = jnp.sum(rd, axis=0, keepdims=True) + own * self.stats_ref[self.i, 2:3, cols]
            rd = rd * inv
            at = part * sizes[0]

            def finish(to, e, dp, scale):
                p = e * scale
                p_ref[to : to + CHUNK] = p.astype(jnp.bfloat16)
                ds_ref[self.h, at + to : at + to + CHUNK] = (p * (dp - rd)).astype(jnp.bfloat16)

            for r in starts:
                finish(r, s_ref[r : r + CHUNK], dp_ref[r : r + CHUNK], inv)
            own = own * inv
            for r in range(0, (part + 1) * half, CHUNK):
                source = slice(part * half + r, part * half + r + CHUNK)
                finish(shared + r, self.e_ref[self.i, source], self.own_dp_ref[self.i, source], own)

        def grads(self, part):
            n = sizes[part]
            at = part * sizes[0]
            self.dv[part] = dot(p_refs[part][:n], self.gs[part], NN)
            self.dk[part] = dot(ds_ref[self.h, at : at + n], self.qs[part], NN)

        def finish(self):
            m = sizes[0]
            dk, dv = (jnp.concatenate([x[0] + x[1][:m], x[1][m:]], 0) for x in (self.dk, self.dv))
            dk = dk * FACTOR
            at = self.at
            dk_ref[:, at] = dk[shared:].astype(jnp.bfloat16)
            dv_ref[:, at] = dv[shared:].astype(jnp.bfloat16)
            for i, o in enumerate(droot_refs):
                r = slice(i * root_half, (i + 1) * root_half)
                o[:, at] = jnp.concatenate([dk[r], dv[r]], 0).astype(jnp.bfloat16)
            for s, o in enumerate(dmid_refs):
                r = slice(root_rows + s * mid_part, root_rows + (s + 1) * mid_part)
                o[:, at] = jnp.concatenate([dk[r], dv[r]], 0).astype(jnp.bfloat16)

    @pl.loop(0, pairs)
    def two_heads(i):
        a, b = Head(i, 0), Head(i, 1)
        a.scores(0)
        a.scores(1)
        a.softmax(0)
        a.grads(0)
        b.scores(0)
        a.softmax(1)
        a.grads(1)
        b.scores(1)
        b.softmax(0)
        a.finish()
        b.grads(0)
        b.softmax(1)
        b.grads(1)
        b.finish()


def query_grads_kernel(heads_per, first, count, half, carried, _, keys_ref, ds_ref, *refs):
    dq_hbm, dq_ref, sems, carried_sems = refs[-4 - carried], *refs[-3:]
    n_all = keys_ref.shape[1]
    span = heads_per * HD
    moves = [
        pltpu.make_async_copy(refs[i], refs[i - 3 - carried], carried_sems.at[i]) for i in range(carried)
    ]
    for c in moves:
        c.start()

    def copy_out(i):
        at = pl.ds(pl.multiple_of(i * span, span), span)
        to = pl.ds(pl.multiple_of((i + first) * span, span), span)
        return pltpu.make_async_copy(dq_ref.at[:, at], dq_hbm.at[:, to], sems.at[i])

    @pl.loop(0, count)
    def one_head(i):
        keys = keys_ref[i + first]
        start = 0
        for part in range(2):
            n = n_all - (1 - part) * half
            dq = dot(keys[:n], ds_ref[i + first, start : start + n], TN)
            dq = (dq * FACTOR).T.astype(jnp.bfloat16)
            start += n
            for g in range(heads_per):
                at = pl.ds(pl.multiple_of(i * span + g * HD, HD), HD)
                dq_ref[part * half : (part + 1) * half, at] = dq[g * half : (g + 1) * half]
        copy_out(i).start()

    for c in moves:
        c.wait()
    for i in range(count):
        copy_out(i).wait()


def cost(matmuls, key_rows, queries, nbytes):
    rows, cols = queries.shape
    return pl.CostEstimate(
        flops=2 * matmuls * rows * key_rows * cols,
        bytes_accessed=nbytes,
        transcendentals=rows * key_rows * cols // HD,
    )


def in_hbm(*arrays):
    return [pltpu.with_memory_space_constraint(x, pltpu.HBM) for x in arrays]


ANY = pl.BlockSpec(memory_space=pl.ANY)
VMEM = pl.BlockSpec(memory_space=pltpu.VMEM)
SMEM = pl.BlockSpec(memory_space=pltpu.SMEM)


def own_part(parity, first, queries, out_grad, leaf_keys, leaf_values):
    rows, cols = leaf_keys.shape
    count = cols // (2 * HD)
    span = queries.shape[1] // cols * HD
    lanes = span // HD * rows // 2
    bf, f32 = jnp.bfloat16, jnp.float32
    shapes = [((rows, span), bf)] * 2 + [((rows, HD), bf)] * 2
    shapes += [((3 * rows // 2, lanes), f32)] * 2 + [((8, 2 * lanes), f32)]
    return pl.pallas_call(
        functools.partial(own_kernel, parity),
        in_specs=[ANY] * 5,
        out_specs=[VMEM] * len(shapes),
        out_shape=[jax.ShapeDtypeStruct((count,) + s, t) for s, t in shapes],
        scratch_shapes=[pltpu.SemaphoreType.DMA((count, 4))],
        compiler_params=pltpu.CompilerParams(vmem_limit_bytes=16 << 20),
        cost_estimate=cost(1, rows, queries, 2 * queries.size),
    )(first, *in_hbm(queries, out_grad, leaf_keys, leaf_values))


def terms_part(where, mid_len, leaf_len, slots, own, blocks, roots, mid_part):
    pairs, leaf_rows, span = own[0][0].shape
    cols = blocks[0].shape[1]
    heads = 2 * pairs
    shared = slots * mid_part + roots[0].shape[0]
    key_rows = shared + leaf_rows
    half = leaf_rows // 2
    lanes = span // HD * half
    bf, f32 = jnp.bfloat16, jnp.float32
    shapes = [
        (heads, key_rows, HD),
        (heads, 2 * key_rows - half, lanes),
        (leaf_rows, cols),
        (leaf_rows, cols),
    ]
    shapes += [(2 * mid_part, cols)] * slots + [x.shape for x in roots]
    out = pl.pallas_call(
        functools.partial(terms_kernel, slots, mid_part),
        in_specs=[SMEM] * 3 + [VMEM] * (16 + len(blocks)),
        out_specs=[VMEM] * len(shapes),
        out_shape=[jax.ShapeDtypeStruct(s, bf) for s in shapes],
        scratch_shapes=[pltpu.VMEM((shared, lanes), f32) for _ in range(4)]
        + [pltpu.VMEM((key_rows, lanes), bf) for _ in range(2)],
        compiler_params=pltpu.CompilerParams(vmem_limit_bytes=(14 if shared <= 256 else 40) << 20),
        cost_estimate=pl.CostEstimate(
            flops=8 * leaf_rows * key_rows * span * heads,
            bytes_accessed=4 * leaf_rows * span * heads,
            transcendentals=leaf_rows * key_rows * heads,
        ),
    )(where, mid_len, leaf_len, *own[0], *own[1], *blocks, *roots)
    return out[0], out[1], out[2:4], out[4 : 4 + slots], out[4 + slots :]


def query_grads(after_this, first, count, so_far, queries, keys, ds, carried=()):
    rows, cols = queries.shape
    heads = keys.shape[0]
    heads_per = cols // (heads * HD)
    like = [jax.ShapeDtypeStruct(x.shape, x.dtype) for x in (queries, *carried)]
    return pl.pallas_call(
        functools.partial(query_grads_kernel, heads_per, first, count, rows // 2, len(carried)),
        in_specs=[ANY] + [VMEM] * (2 + len(carried)) + [ANY] * len(so_far),
        out_specs=[ANY] * len(like),
        out_shape=like,
        input_output_aliases={3 + len(carried) + i: i for i in range(len(so_far))},
        scratch_shapes=[
            pltpu.VMEM((rows, count * heads_per * HD), jnp.bfloat16),
            pltpu.SemaphoreType.DMA((count,)),
            pltpu.SemaphoreType.DMA((max(len(carried), 1),)),
        ],
        compiler_params=pltpu.CompilerParams(
            vmem_limit_bytes=(10 if keys.shape[1] <= 512 else 32) << 20
        ),
        cost_estimate=cost(1, keys.shape[1] * count // heads, queries, 2 * queries.size),
    )(after_this, keys, ds, *carried, *so_far)


def gather_kernel(mk_ref, mv_ref, rk_ref, rv_ref, mid_ref, pair_ref):
    mid_ref[...] = jnp.concatenate([mk_ref[...], mv_ref[...]], 0)
    pair_ref[...] = jnp.concatenate([rk_ref[...], rv_ref[...]], 0)


def gather_own(mid_keys, mid_values, root_keys, root_values):
    return pl.pallas_call(
        gather_kernel,
        out_shape=[
            jax.ShapeDtypeStruct((2 * x.shape[0], x.shape[1]), x.dtype)
            for x in (mid_keys, root_keys)
        ],
        compiler_params=pltpu.CompilerParams(vmem_limit_bytes=4 << 20),
    )(*in_hbm(mid_keys, mid_values, root_keys, root_values))


def pack_kernel(root_own, where_ref, mid_len_ref, leaf_len_ref, mid_ref, *refs):
    pairs = [r[...].astype(jnp.float32) for r in refs[:-1]]
    roots = [p[:root_own] for p in pairs] + [p[root_own:] for p in pairs]
    refs[-1][...] = jnp.concatenate(
        [mid_ref[...], jnp.concatenate(roots, 0).astype(jnp.bfloat16)], 0
    )


def pack(scalars, mid, pairs):
    rows = mid.shape[0] + len(pairs) * pairs[0].shape[0]
    return pl.pallas_call(
        functools.partial(pack_kernel, pairs[0].shape[0] // 2),
        in_specs=[SMEM] * 3 + [VMEM] * (1 + len(pairs)),
        out_shape=jax.ShapeDtypeStruct((rows, mid.shape[1]), jnp.bfloat16),
        compiler_params=pltpu.CompilerParams(vmem_limit_bytes=4 << 20),
    )(*scalars, mid, *pairs)


def join_kernel(mid_rows, _, a_ref, b_ref, out_ref):
    rows = a_ref.shape[0]
    out_ref[:mid_rows] = a_ref[:mid_rows]
    out_ref[mid_rows : 2 * mid_rows] = b_ref[:mid_rows]
    roots = [r[mid_rows:rows].astype(jnp.float32) for r in (a_ref, b_ref)]
    out_ref[2 * mid_rows :] = jnp.concatenate(roots, 0).astype(jnp.bfloat16)


def join(first, a, b, mid_rows):
    return pl.pallas_call(
        functools.partial(join_kernel, mid_rows),
        out_shape=jax.ShapeDtypeStruct((2 * a.shape[0], a.shape[1]), a.dtype),
        compiler_params=pltpu.CompilerParams(vmem_limit_bytes=4 << 20),
    )(first, a, b)


def root_of(ref, mid_rows, place):
    if place is None:
        return ref[mid_rows:].astype(jnp.float32)
    both = ref[2 * mid_rows :].astype(jnp.float32)
    rows = both.shape[0] // 2
    return both[place * rows : (place + 1) * rows]


def two_level(slots):
    found = places(slots)
    return [(i, j if slots >= 4 and i == 2 else None) for i, j in found]


def collect_kernel(slots, mid_rows, _, *refs):
    out_ref = refs[-1]
    roots = [root_of(refs[i], mid_rows, j) for i, j in two_level(slots)]
    half = roots[0].shape[0] // 2
    out_ref[...] = jnp.concatenate(
        [r[:half] for r in roots] + [r[half:] for r in roots], 0
    ).astype(jnp.bfloat16)


def collect(first, blocks, slots, mid_rows):
    rows = slots * (blocks[0].shape[0] - mid_rows)
    return pl.pallas_call(
        functools.partial(collect_kernel, slots, mid_rows),
        in_specs=[ANY] + [VMEM] * len(blocks),
        out_shape=jax.ShapeDtypeStruct((rows, blocks[0].shape[1]), jnp.bfloat16),
        compiler_params=pltpu.CompilerParams(vmem_limit_bytes=8 << 20),
    )(first, *blocks)


def spread_kernel(slots, mid_rows, a_ref, b_ref, *refs):
    mids, outs = refs[:slots], refs[slots:]
    total = a_ref[...].astype(jnp.float32) + b_ref[...].astype(jnp.float32)
    half = total.shape[0] // 2
    part = half // slots
    roots = [
        jnp.concatenate([total[at + s * part : at + (s + 1) * part] for at in (0, half)], 0)
        for s in range(slots)
    ]
    held = {}
    for s, (i, j) in enumerate(two_level(slots)):
        at = mid_rows * (j or 0)
        outs[i][at : at + mid_rows] = mids[s][...]
        held.setdefault(i, []).append(roots[s])
    for i, x in held.items():
        outs[i][len(x) * mid_rows :] = jnp.concatenate(x, 0).astype(jnp.bfloat16)


def spread(a, b, mids):
    slots = len(mids)
    mid_rows, cols = mids[0].shape
    rows = mid_rows + a.shape[0] // slots
    arrays = places(slots)[-1][0] + 1
    shapes = [(2 * rows if slots >= 4 and i == 2 else rows, cols) for i in range(arrays)]
    return pl.pallas_call(
        functools.partial(spread_kernel, slots, mid_rows),
        out_shape=[jax.ShapeDtypeStruct(x, jnp.bfloat16) for x in shapes],
        compiler_params=pltpu.CompilerParams(vmem_limit_bytes=8 << 20),
    )(a, b, *mids)


def near_sum_kernel(mid_rows, a_ref, pair_ref, out_ref):
    pair = pair_ref[mid_rows : 2 * mid_rows].astype(jnp.float32)
    out_ref[:mid_rows] = (a_ref[:mid_rows].astype(jnp.float32) + pair).astype(jnp.bfloat16)
    root = root_of(a_ref, mid_rows, None) + root_of(pair_ref, mid_rows, 1)
    out_ref[mid_rows:] = root.astype(jnp.bfloat16)


def near_sum(a, pair, mid_rows):
    return pl.pallas_call(
        functools.partial(near_sum_kernel, mid_rows),
        out_shape=jax.ShapeDtypeStruct(a.shape, a.dtype),
        compiler_params=pltpu.CompilerParams(vmem_limit_bytes=4 << 20),
    )(a, pair)


def far_sum_kernel(_, a_ref, b_ref, out_ref):
    out_ref[...] = (a_ref[...].astype(jnp.float32) + b_ref[...].astype(jnp.float32)).astype(jnp.bfloat16)


def far_sum(first, a, b):
    return pl.pallas_call(
        far_sum_kernel,
        in_specs=[ANY] + [VMEM] * 2,
        out_shape=jax.ShapeDtypeStruct(a.shape, a.dtype),
        compiler_params=pltpu.CompilerParams(vmem_limit_bytes=4 << 20),
    )(first, a, b)


def after_kernel(*refs):
    pass


def after(first, arrays):
    return pl.pallas_call(
        after_kernel,
        in_specs=[VMEM] + [ANY] * len(arrays),
        out_specs=[ANY] * len(arrays),
        out_shape=[jax.ShapeDtypeStruct(x.shape, x.dtype) for x in arrays],
        input_output_aliases={1 + i: i for i in range(len(arrays))},
        compiler_params=pltpu.CompilerParams(vmem_limit_bytes=4 << 20),
    )(first, *arrays)


def mid_sums_kernel(mid_part, *refs):
    for i, o in enumerate(refs[-2:]):
        rows = slice(i * mid_part, (i + 1) * mid_part)
        total = refs[0][rows].astype(jnp.float32)
        for r in refs[1:-2]:
            total = total + r[rows].astype(jnp.float32)
        o[...] = total


def mid_sums(blocks, mid_part):
    return pl.pallas_call(
        functools.partial(mid_sums_kernel, mid_part),
        out_shape=[jax.ShapeDtypeStruct((mid_part, blocks[0].shape[1]), jnp.float32)] * 2,
        compiler_params=pltpu.CompilerParams(vmem_limit_bytes=8 << 20),
    )(*blocks)


def root_sums_kernel(count, mid_rows, root_own, paired, _, *refs):
    root = None
    for i, r in enumerate(refs[:count]):
        x = root_of(r, mid_rows, 0 if paired and i == 1 else None)
        root = x if root is None else root + x
    half = root.shape[0] // 2
    for t, o in enumerate(refs[count:]):
        o[:root_own] = root[t * root_own : (t + 1) * root_own]
        o[root_own:] = root[half + t * root_own : half + (t + 1) * root_own]


def root_sums(first, blocks, mid_rows, root_own, pieces):
    shape = jax.ShapeDtypeStruct((2 * root_own, blocks[0].shape[1]), jnp.float32)
    paired = blocks[1].shape[0] > blocks[0].shape[0]
    return pl.pallas_call(
        functools.partial(root_sums_kernel, len(blocks), mid_rows, root_own, paired),
        in_specs=[ANY] + [VMEM] * len(blocks),
        out_shape=[shape] * pieces,
        compiler_params=pltpu.CompilerParams(vmem_limit_bytes=8 << 20),
    )(*in_hbm(first), *blocks)


def root_kernel(root_own, *refs):
    total = refs[0][...]
    for r in refs[1:-2]:
        total = total + r[...]
    refs[-2][...] = total[:root_own]
    refs[-1][...] = total[root_own:]


def add_roots(pieces):
    rows, cols = pieces[0].shape
    return pl.pallas_call(
        functools.partial(root_kernel, rows // 2),
        out_shape=[jax.ShapeDtypeStruct((rows // 2, cols), jnp.float32)] * 2,
        compiler_params=pltpu.CompilerParams(vmem_limit_bytes=4 << 20),
    )(*pieces)


def swap(x, axis, size, offset):
    return lax.ppermute(x, axis, [(i, i ^ offset) for i in range(size)])


def on_device(
    mids,
    leaves,
    queries,
    out_grad,
    leaf_keys,
    leaf_values,
    mid_keys,
    mid_values,
    root_keys,
    root_values,
    mid_len,
    leaf_len,
):
    mid_part = mid_keys.shape[0]
    root_own = root_keys.shape[0]
    where = lax.axis_index("leaf").reshape(1).astype(jnp.int32)
    mid, pair = gather_own(mid_keys, mid_values, root_keys, root_values)
    mid_rows = 2 * mid_part
    same_core = range(2, mids, 2)
    pairs = [pair] + [swap(pair, "mid", mids, t) for t in same_core]
    block = pack((where, mid_len, leaf_len), mid, pairs)

    def leaf_swap(x, s):
        return swap(x, "leaf", leaves, s)

    far = list(reversed(range(4, leaves, 2)))
    far_blocks = [leaf_swap(block, s) for s in far]
    beside = leaf_swap(block, 1)
    operands = (queries, out_grad, leaf_keys, leaf_values)
    own = [own_part(0, block, *operands)]
    token = own[0][-1]
    near = leaf_swap(join(token, block, beside, mid_rows), 2)
    far_blocks = after(token, far_blocks)
    own.append(own_part(1, far_blocks[-1] if far else token, *operands))
    blocks = [block, beside, near]
    for x in reversed(far_blocks):
        blocks += [x, leaf_swap(x, 1)]
    root = collect(own[1][-1], blocks, leaves, mid_rows)
    roots = [root, swap(root, "mid", mids, 1)]
    keys, ds, leaf_grads, mid_terms, root_terms = terms_part(
        where, mid_len, leaf_len, leaves, own, blocks, roots, mid_part
    )

    terms = spread(root_terms[0], swap(root_terms[1], "mid", mids, 1), mid_terms)
    through = [leaf_swap(terms[s], 1) for s in far]
    near = leaf_swap(terms[2], 2)
    heads = leaf_keys.shape[1] // HD
    early = heads // 2
    query_grad, *leaf_grads = query_grads(terms[0], 0, early, (), queries, keys, ds, leaf_grads)
    leaf_key_grad, leaf_value_grad = leaf_grads
    token = in_hbm(leaf_value_grad)[0]
    arrived = [terms[0], near]
    for s, x in zip(far, through):
        arrived.append(leaf_swap(far_sum(token, terms[s - 1], x), s))
    arrived.append(leaf_swap(near_sum(terms[1], near, mid_rows), 1))
    (query_grad,) = query_grads(terms[0], early, heads - early, (query_grad,), queries, keys, ds)
    pieces = root_sums(query_grad, arrived, mid_rows, root_own, mids // 2)
    mid_key_grad, mid_value_grad = mid_sums(arrived, mid_part)
    pieces = [pieces[0]] + [swap(x, "mid", mids, t) for t, x in zip(same_core, pieces[1:])]
    root_key_grad, root_value_grad = add_roots(pieces)
    return (
        query_grad,
        leaf_key_grad,
        leaf_value_grad,
        mid_key_grad,
        mid_value_grad,
        root_key_grad,
        root_value_grad,
    )


def solution(mesh):
    both = P(("mid", "leaf"), None)
    in_specs = (both,) * 8 + (P("mid"), P(("mid", "leaf")))
    return jax.shard_map(
        functools.partial(on_device, mesh.shape["mid"], mesh.shape["leaf"]),
        mesh=mesh,
        in_specs=in_specs,
        out_specs=(both,) * 7,
        check_vma=False,
    )
```

```python
import functools
import math

import jax
import jax.numpy as jnp
from jax import lax
from jax.experimental import pallas as pl
from jax.experimental.pallas import tpu as pltpu
from jax.sharding import PartitionSpec as P

HD = 128
FACTOR = HD**-0.5
LOG2E = math.log2(math.e)
CHUNK = 16
NEG = -1e30
NT = (((1,), (1,)), ((), ()))
NN = (((1,), (0,)), ((), ()))
TN = (((0,), (0,)), ((), ()))


def dot(a, b, dims):
    return lax.dot_general(a, b, dims, preferred_element_type=jnp.float32)


def stacked(ref, part, half, heads_per):
    rows = slice(part * half, (part + 1) * half)
    return jnp.concatenate([ref[rows, h * HD : (h + 1) * HD] for h in range(heads_per)], 0)


def fold(x):
    return [x[i : i + 8] for i in range(0, x.shape[0], 8)]


def total_of(so_far, x, op):
    for y in fold(x):
        so_far = y if so_far is None else op(so_far, y)
    return so_far


def own_kernel(
    parity, _, q_hbm, g_hbm, k_hbm, v_hbm, q_ref, g_ref, k_ref, v_ref, e_ref, dp_ref, stats_ref, sems
):
    count, leaf_rows, span = q_ref.shape
    half = leaf_rows // 2
    heads_per = span // HD
    lanes = heads_per * half

    def copies(i):
        h = 2 * i + parity
        wide = pl.ds(pl.multiple_of(h * span, span), span)
        at = pl.ds(pl.multiple_of(h * HD, HD), HD)
        pairs = [
            (q_hbm.at[:, wide], q_ref.at[i]),
            (g_hbm.at[:, wide], g_ref.at[i]),
            (k_hbm.at[:, at], k_ref.at[i]),
            (v_hbm.at[:, at], v_ref.at[i]),
        ]
        return [pltpu.make_async_copy(x, y, sems.at[i, j]) for j, (x, y) in enumerate(pairs)]

    for i in range(count):
        for c in copies(i):
            c.start()
    chunk_row = lax.broadcasted_iota(jnp.int32, (CHUNK, half), 0)
    chunk_col = lax.broadcasted_iota(jnp.int32, (CHUNK, half), 1)

    @pl.loop(0, count)
    def one_head(i):
        for c in copies(i):
            c.wait()

        def scores(part):
            n, at = (part + 1) * half, part * half
            e_ref[i, at : at + n] = dot(k_ref[i, :n], stacked(q_ref.at[i], part, half, heads_per), NT)
            dp_ref[i, at : at + n] = dot(v_ref[i, :n], stacked(g_ref.at[i], part, half, heads_per), NT)

        def softmax(part):
            n, at = (part + 1) * half, part * half
            cols = slice(part * lanes, (part + 1) * lanes)

            def masked_chunk(r):
                s = e_ref[i, at + r : at + r + CHUNK]
                if r < n - half:
                    return s
                mask = chunk_row + (r - n + half) <= chunk_col
                return jnp.concatenate(
                    [jnp.where(mask, s[:, g * half : (g + 1) * half], NEG) for g in range(heads_per)], 1
                )

            starts = range(0, n, CHUNK)
            top = total = rd = None
            for r in starts:
                top = total_of(top, masked_chunk(r), jnp.maximum)
            top = jnp.max(top, axis=0, keepdims=True)
            for r in starts:
                e = jnp.exp2((masked_chunk(r) - top) * (FACTOR * LOG2E))
                e_ref[i, at + r : at + r + CHUNK] = e
                total = total_of(total, e, jnp.add)
                rd = total_of(rd, e * dp_ref[i, at + r : at + r + CHUNK], jnp.add)
            stats_ref[i, 0:1, cols] = top
            stats_ref[i, 1:2, cols] = jnp.sum(total, axis=0, keepdims=True)
            stats_ref[i, 2:3, cols] = jnp.sum(rd, axis=0, keepdims=True)

        scores(0)
        scores(1)
        softmax(0)
        softmax(1)


def places(slots):
    if slots < 4:
        return [(s, None) for s in range(slots)]
    found = [(0, None), (1, None), (2, 0), (2, 1)]
    for n in range(3, 3 * slots // 4, 3):
        found += [(n, None), (n + 2, 0), (n + 1, None), (n + 2, 1)]
    return found


def arrays_of(slots):
    return max(i for i, _ in places(slots)) + 1


def terms_kernel(slots, mid_part, where_ref, mid_len_ref, leaf_len_ref, *refs):
    own_parts = refs[:7], refs[7:14]
    arrays = arrays_of(slots)
    block_refs = [
        refs[14 + i].at[pl.ds((j or 0) * 2 * mid_part, 2 * mid_part)] for i, j in places(slots)
    ]
    root_refs = refs[14 + arrays : 16 + arrays]
    outs = refs[16 + arrays :]
    keys_ref, ds_ref, own_p_ref = outs[:3]
    dmid_refs = outs[3 : 3 + slots]
    droot_refs = outs[3 + slots : 5 + slots]
    s_refs, dp_refs, p_refs = (outs[5 + slots + 2 * i : 7 + slots + 2 * i] for i in range(3))
    root_half = root_refs[0].shape[0] // 2
    me = where_ref[0]
    mid_live = mid_len_ref[0]
    leaf_live = leaf_len_ref[0]
    pairs, leaf_rows, span = own_parts[0][0].shape
    half = leaf_rows // 2
    heads_per = span // HD
    mid_rows = slots * mid_part
    root_rows = 2 * root_half
    shared = root_rows + mid_rows
    lanes = heads_per * half
    sizes = [shared + half, shared + 2 * half]
    chunk_row = lax.broadcasted_iota(jnp.int32, (CHUNK, half), 0)
    lane = lax.broadcasted_iota(jnp.int32, (1, half), 1)

    def live(part, x):
        alive = lane + part * half < leaf_live
        return jnp.concatenate(
            [jnp.where(alive, x[:, g * half : (g + 1) * half], 0.0) for g in range(heads_per)], 1
        )

    def masked_chunk(s_ref, r):
        s = s_ref[r : r + CHUNK]
        if r < root_rows:
            return s
        slot, rest = divmod(r - root_rows, mid_part)
        mask = chunk_row < mid_live - rest - jnp.bitwise_xor(me, slot) * mid_part
        return jnp.concatenate(
            [jnp.where(mask, s[:, g * half : (g + 1) * half], NEG) for g in range(heads_per)], 1
        )

    class Head:
        def __init__(self, i, parity):
            self.i = i
            self.h = h = 2 * i + parity
            self.at = pl.ds(pl.multiple_of(h * HD, HD), HD)
            q_ref, g_ref, k_ref, _, self.e_ref, self.own_dp_ref, self.stats_ref = own_parts[parity]
            self.keys = self.whole(0)
            self.values = self.whole(1)
            keys_ref[h, :shared] = self.keys
            keys_ref[h, shared:] = k_ref[i]
            self.qs = [stacked(q_ref.at[i], p, half, heads_per) for p in range(2)]
            self.gs = [stacked(g_ref.at[i], p, half, heads_per) for p in range(2)]
            self.dk, self.dv = [None, None], [None, None]

        def whole(self, which):
            at = self.at
            roots = [r[which * root_half : (which + 1) * root_half, at] for r in root_refs]
            mids = [r[which * mid_part : (which + 1) * mid_part, at] for r in block_refs]
            return jnp.concatenate(roots + mids, 0)

        def scores(self, part):
            s_refs[part][...] = dot(self.keys, self.qs[part], NT)
            dp_refs[part][...] = dot(self.values, self.gs[part], NT)

        def softmax(self, part):
            s_ref, dp_ref, p_ref = s_refs[part], dp_refs[part], p_refs[part]
            cols = slice(part * lanes, (part + 1) * lanes)
            own_top = self.stats_ref[self.i, 0:1, cols]
            top = total = rd = None
            starts = range(0, shared, CHUNK)
            for r in starts:
                top = total_of(top, masked_chunk(s_ref, r), jnp.maximum)
            top = jnp.maximum(jnp.max(top, axis=0, keepdims=True), own_top)
            own = jnp.exp2((own_top - top) * (FACTOR * LOG2E))
            for r in starts:
                e = jnp.exp2((masked_chunk(s_ref, r) - top) * (FACTOR * LOG2E))
                s_ref[r : r + CHUNK] = e
                total = total_of(total, e, jnp.add)
                rd = total_of(rd, e * dp_ref[r : r + CHUNK], jnp.add)
            total = jnp.sum(total, axis=0, keepdims=True) + own * self.stats_ref[self.i, 1:2, cols]
            inv = live(part, 1.0 / total)
            rd = jnp.sum(rd, axis=0, keepdims=True) + own * self.stats_ref[self.i, 2:3, cols]
            rd = rd * inv
            at = part * sizes[0]

            def finish(at, e, dp, scale, p_out, p_at):
                p = e * scale
                p_out[p_at : p_at + CHUNK] = p.astype(jnp.bfloat16)
                ds_ref[self.h, at : at + CHUNK] = (p * (dp - rd)).astype(jnp.bfloat16)

            for r in starts:
                finish(at + r, s_ref[r : r + CHUNK], dp_ref[r : r + CHUNK], inv, p_ref, r)
            own = own * inv
            for r in range(0, (part + 1) * half, CHUNK):
                to = part * half + r
                source = slice(to, to + CHUNK)
                e, dp = self.e_ref[self.i, source], self.own_dp_ref[self.i, source]
                finish(at + shared + r, e, dp, own, own_p_ref.at[self.h], to)

        def grads(self, part):
            at = part * sizes[0]
            self.dv[part] = dot(p_refs[part][...], self.gs[part], NN)
            self.dk[part] = dot(ds_ref[self.h, at : at + shared], self.qs[part], NN)

        def finish(self):
            dv = self.dv[0] + self.dv[1]
            dk = (self.dk[0] + self.dk[1]) * FACTOR
            at = self.at
            for i, o in enumerate(droot_refs):
                r = slice(i * root_half, (i + 1) * root_half)
                o[:, at] = jnp.concatenate([dk[r], dv[r]], 0).astype(jnp.bfloat16)
            for s, o in enumerate(dmid_refs):
                r = slice(root_rows + s * mid_part, root_rows + (s + 1) * mid_part)
                o[:, at] = jnp.concatenate([dk[r], dv[r]], 0).astype(jnp.bfloat16)

    @pl.loop(0, pairs)
    def two_heads(i):
        a, b = Head(i, 0), Head(i, 1)
        a.scores(0)
        a.scores(1)
        a.softmax(0)
        a.grads(0)
        b.scores(0)
        a.softmax(1)
        a.grads(1)
        b.scores(1)
        b.softmax(0)
        a.finish()
        b.grads(0)
        b.softmax(1)
        b.grads(1)
        b.finish()


def query_grads_kernel(heads_per, first, count, half, _, keys_ref, ds_ref, *refs):
    dq_hbm, dq_ref, sems = refs[-3:]
    n_all = keys_ref.shape[1]
    span = heads_per * HD

    def copy_out(i):
        at = pl.ds(pl.multiple_of(i * span, span), span)
        to = pl.ds(pl.multiple_of((i + first) * span, span), span)
        return pltpu.make_async_copy(dq_ref.at[:, at], dq_hbm.at[:, to], sems.at[i])

    @pl.loop(0, count)
    def one_head(i):
        keys = keys_ref[i + first]
        start = 0
        for part in range(2):
            n = n_all - (1 - part) * half
            dq = dot(keys[:n], ds_ref[i + first, start : start + n], TN)
            dq = (dq * FACTOR).T.astype(jnp.bfloat16)
            start += n
            for g in range(heads_per):
                at = pl.ds(pl.multiple_of(i * span + g * HD, HD), HD)
                dq_ref[part * half : (part + 1) * half, at] = dq[g * half : (g + 1) * half]
        copy_out(i).start()

    for i in range(count):
        copy_out(i).wait()


def own_grads_kernel(_, q0_ref, g0_ref, q1_ref, g1_ref, p_ref, ds_ref, dk_hbm, dv_hbm, dk_ref, dv_ref, sems):
    pairs, leaf_rows, span = q0_ref.shape
    half = leaf_rows // 2
    heads_per = span // HD
    first = ds_ref.shape[1] // 2 - half // 2

    def copies_out(h):
        at = pl.ds(pl.multiple_of(h * HD, HD), HD)
        return [
            pltpu.make_async_copy(x.at[:, at], y.at[:, at], sems.at[h, j])
            for j, (x, y) in enumerate(((dk_ref, dk_hbm), (dv_ref, dv_hbm)))
        ]

    @pl.loop(0, pairs)
    def two_heads(i):
        for parity, (q_ref, g_ref) in enumerate(((q0_ref, g0_ref), (q1_ref, g1_ref))):
            h = 2 * i + parity
            at = pl.ds(pl.multiple_of(h * HD, HD), HD)
            dk, dv = [], []
            for part in range(2):
                n = (part + 1) * half
                end = first if part == 0 else ds_ref.shape[1]
                qs = stacked(q_ref.at[i], part, half, heads_per)
                gs = stacked(g_ref.at[i], part, half, heads_per)
                dv.append(dot(p_ref[h, part * half : part * half + n], gs, NN))
                dk.append(dot(ds_ref[h, end - n : end], qs, NN))
            for x, ref, scale in ((dk, dk_ref, FACTOR), (dv, dv_ref, 1.0)):
                ref[:half, at] = ((x[0] + x[1][:half]) * scale).astype(jnp.bfloat16)
                ref[half:, at] = (x[1][half:] * scale).astype(jnp.bfloat16)
            for c in copies_out(h):
                c.start()

    for h in range(2 * pairs):
        for c in copies_out(h):
            c.wait()


def cost(matmuls, key_rows, queries, nbytes):
    rows, cols = queries.shape
    return pl.CostEstimate(
        flops=2 * matmuls * rows * key_rows * cols,
        bytes_accessed=nbytes,
        transcendentals=rows * key_rows * cols // HD,
    )


def in_hbm(*arrays):
    return [pltpu.with_memory_space_constraint(x, pltpu.HBM) for x in arrays]


ANY = pl.BlockSpec(memory_space=pl.ANY)
VMEM = pl.BlockSpec(memory_space=pltpu.VMEM)
SMEM = pl.BlockSpec(memory_space=pltpu.SMEM)


def own_part(parity, first, queries, out_grad, leaf_keys, leaf_values):
    rows, cols = leaf_keys.shape
    count = cols // (2 * HD)
    span = queries.shape[1] // cols * HD
    lanes = span // HD * rows // 2
    bf, f32 = jnp.bfloat16, jnp.float32
    shapes = [((rows, span), bf)] * 2 + [((rows, HD), bf)] * 2
    shapes += [((3 * rows // 2, lanes), f32)] * 2 + [((8, 2 * lanes), f32)]
    return pl.pallas_call(
        functools.partial(own_kernel, parity),
        in_specs=[ANY] * 5,
        out_specs=[VMEM] * len(shapes),
        out_shape=[jax.ShapeDtypeStruct((count,) + s, t) for s, t in shapes],
        scratch_shapes=[pltpu.SemaphoreType.DMA((count, 4))],
        compiler_params=pltpu.CompilerParams(vmem_limit_bytes=16 << 20),
        cost_estimate=cost(1, rows, queries, 2 * queries.size),
    )(first, *in_hbm(queries, out_grad, leaf_keys, leaf_values))


def terms_part(where, mid_len, leaf_len, slots, own, blocks, roots, mid_part):
    pairs, leaf_rows, span = own[0][0].shape
    cols = blocks[0].shape[1]
    heads = 2 * pairs
    shared = slots * mid_part + roots[0].shape[0]
    key_rows = shared + leaf_rows
    half = leaf_rows // 2
    lanes = span // HD * half
    bf, f32 = jnp.bfloat16, jnp.float32
    shapes = [
        (heads, key_rows, HD),
        (heads, 2 * key_rows - half, lanes),
        (heads, 3 * half, lanes),
    ]
    shapes += [(2 * mid_part, cols)] * slots + [x.shape for x in roots]
    out = pl.pallas_call(
        functools.partial(terms_kernel, slots, mid_part),
        in_specs=[SMEM] * 3 + [VMEM] * (16 + len(blocks)),
        out_specs=[VMEM] * len(shapes),
        out_shape=[jax.ShapeDtypeStruct(s, bf) for s in shapes],
        scratch_shapes=[pltpu.VMEM((shared, lanes), f32) for _ in range(4)]
        + [pltpu.VMEM((shared, lanes), bf) for _ in range(2)],
        compiler_params=pltpu.CompilerParams(vmem_limit_bytes=(14 if shared <= 256 else 52) << 20),
        cost_estimate=pl.CostEstimate(
            flops=8 * leaf_rows * key_rows * span * heads,
            bytes_accessed=4 * leaf_rows * span * heads,
            transcendentals=leaf_rows * key_rows * heads,
        ),
    )(where, mid_len, leaf_len, *own[0], *own[1], *blocks, *roots)
    return out[0], out[1], out[2], out[3 : 3 + slots], out[3 + slots :]


def query_grads(after_this, first, count, so_far, queries, keys, ds):
    rows, cols = queries.shape
    heads = keys.shape[0]
    heads_per = cols // (heads * HD)
    return pl.pallas_call(
        functools.partial(query_grads_kernel, heads_per, first, count, rows // 2),
        in_specs=[ANY] + [VMEM] * 2 + [ANY] * len(so_far),
        out_specs=ANY,
        out_shape=jax.ShapeDtypeStruct(queries.shape, jnp.bfloat16),
        input_output_aliases={3 + i: i for i in range(len(so_far))},
        scratch_shapes=[
            pltpu.VMEM((rows, count * heads_per * HD), jnp.bfloat16),
            pltpu.SemaphoreType.DMA((count,)),
        ],
        compiler_params=pltpu.CompilerParams(
            vmem_limit_bytes=(10 if keys.shape[1] <= 512 else 32) << 20
        ),
        cost_estimate=cost(1, keys.shape[1] * count // heads, queries, 2 * queries.size),
    )(after_this, keys, ds, *so_far)


def own_grads(after_this, queries, leaf_keys, own, p, ds):
    heads = p.shape[0]
    shape = jax.ShapeDtypeStruct(leaf_keys.shape, jnp.bfloat16)
    return pl.pallas_call(
        own_grads_kernel,
        in_specs=[ANY] + [VMEM] * 6,
        out_specs=[ANY] * 2,
        out_shape=[shape] * 2,
        scratch_shapes=[pltpu.VMEM(shape.shape, shape.dtype)] * 2
        + [pltpu.SemaphoreType.DMA((heads, 2))],
        compiler_params=pltpu.CompilerParams(
            vmem_limit_bytes=(10 if ds.shape[1] <= 1024 else 52) << 20
        ),
        cost_estimate=cost(2, leaf_keys.shape[0], queries, 2 * queries.size),
    )(*in_hbm(after_this), *own[0][:2], *own[1][:2], p, ds)


def gather_kernel(mk_ref, mv_ref, rk_ref, rv_ref, mid_ref, pair_ref):
    mid_ref[...] = jnp.concatenate([mk_ref[...], mv_ref[...]], 0)
    pair_ref[...] = jnp.concatenate([rk_ref[...], rv_ref[...]], 0)


def gather_own(mid_keys, mid_values, root_keys, root_values):
    return pl.pallas_call(
        gather_kernel,
        out_shape=[
            jax.ShapeDtypeStruct((2 * x.shape[0], x.shape[1]), x.dtype)
            for x in (mid_keys, root_keys)
        ],
        compiler_params=pltpu.CompilerParams(vmem_limit_bytes=4 << 20),
    )(*in_hbm(mid_keys, mid_values, root_keys, root_values))


def pack_kernel(root_own, where_ref, mid_len_ref, leaf_len_ref, mid_ref, *refs):
    pairs = [r[...].astype(jnp.float32) for r in refs[:-1]]
    roots = [p[:root_own] for p in pairs] + [p[root_own:] for p in pairs]
    refs[-1][...] = jnp.concatenate(
        [mid_ref[...], jnp.concatenate(roots, 0).astype(jnp.bfloat16)], 0
    )


def pack(scalars, mid, pairs):
    rows = mid.shape[0] + len(pairs) * pairs[0].shape[0]
    return pl.pallas_call(
        functools.partial(pack_kernel, pairs[0].shape[0] // 2),
        in_specs=[SMEM] * 3 + [VMEM] * (1 + len(pairs)),
        out_shape=jax.ShapeDtypeStruct((rows, mid.shape[1]), jnp.bfloat16),
        compiler_params=pltpu.CompilerParams(vmem_limit_bytes=4 << 20),
    )(*scalars, mid, *pairs)


def join_kernel(mid_rows, _, a_ref, b_ref, out_ref):
    rows = a_ref.shape[0]
    out_ref[:mid_rows] = a_ref[:mid_rows]
    out_ref[mid_rows : 2 * mid_rows] = b_ref[:mid_rows]
    roots = [r[mid_rows:rows].astype(jnp.float32) for r in (a_ref, b_ref)]
    out_ref[2 * mid_rows :] = jnp.concatenate(roots, 0).astype(jnp.bfloat16)


def join(first, a, b, mid_rows):
    return pl.pallas_call(
        functools.partial(join_kernel, mid_rows),
        out_shape=jax.ShapeDtypeStruct((2 * a.shape[0], a.shape[1]), a.dtype),
        compiler_params=pltpu.CompilerParams(vmem_limit_bytes=4 << 20),
    )(first, a, b)


def root_of(ref, mid_rows, place):
    if place is None:
        return ref[mid_rows:].astype(jnp.float32)
    both = ref[2 * mid_rows :].astype(jnp.float32)
    rows = both.shape[0] // 2
    return both[place * rows : (place + 1) * rows]


def collect_kernel(slots, mid_rows, _, *refs):
    out_ref = refs[-1]
    roots = [root_of(refs[i], mid_rows, j) for i, j in places(slots)]
    half = roots[0].shape[0] // 2
    out_ref[...] = jnp.concatenate(
        [r[:half] for r in roots] + [r[half:] for r in roots], 0
    ).astype(jnp.bfloat16)


def collect(first, blocks, slots, mid_rows):
    rows = slots * (blocks[0].shape[0] - mid_rows)
    return pl.pallas_call(
        functools.partial(collect_kernel, slots, mid_rows),
        in_specs=[ANY] + [VMEM] * len(blocks),
        out_shape=jax.ShapeDtypeStruct((rows, blocks[0].shape[1]), jnp.bfloat16),
        compiler_params=pltpu.CompilerParams(vmem_limit_bytes=8 << 20),
    )(first, *blocks)


def spread_kernel(slots, mid_rows, _, a_ref, b_ref, *refs):
    mids, outs = refs[:slots], refs[slots:]
    total = a_ref[...].astype(jnp.float32) + b_ref[...].astype(jnp.float32)
    half = total.shape[0] // 2
    part = half // slots
    roots = [
        jnp.concatenate([total[at + s * part : at + (s + 1) * part] for at in (0, half)], 0)
        for s in range(slots)
    ]
    held = {}
    for s, (i, j) in enumerate(places(slots)):
        at = mid_rows * (j or 0)
        outs[i][at : at + mid_rows] = mids[s][...]
        held.setdefault(i, []).append(roots[s])
    for i, x in held.items():
        outs[i][len(x) * mid_rows :] = jnp.concatenate(x, 0).astype(jnp.bfloat16)


def spread(first, a, b, mids):
    slots = len(mids)
    mid_rows, cols = mids[0].shape
    rows = mid_rows + a.shape[0] // slots
    arrays = arrays_of(slots)
    paired = {i for i, j in places(slots) if j is not None}
    shapes = [(2 * rows if i in paired else rows, cols) for i in range(arrays)]
    return pl.pallas_call(
        functools.partial(spread_kernel, slots, mid_rows),
        in_specs=[ANY] + [VMEM] * (2 + slots),
        out_shape=[jax.ShapeDtypeStruct(x, jnp.bfloat16) for x in shapes],
        compiler_params=pltpu.CompilerParams(vmem_limit_bytes=8 << 20),
    )(*in_hbm(first), a, b, *mids)


def near_sum_kernel(mid_rows, _, a_ref, pair_ref, out_ref):
    pair = pair_ref[mid_rows : 2 * mid_rows].astype(jnp.float32)
    out_ref[:mid_rows] = (a_ref[:mid_rows].astype(jnp.float32) + pair).astype(jnp.bfloat16)
    root = root_of(a_ref, mid_rows, None) + root_of(pair_ref, mid_rows, 1)
    out_ref[mid_rows:] = root.astype(jnp.bfloat16)


def near_sum(first, a, pair, mid_rows):
    return pl.pallas_call(
        functools.partial(near_sum_kernel, mid_rows),
        in_specs=[ANY] + [VMEM] * 2,
        out_shape=jax.ShapeDtypeStruct(a.shape, a.dtype),
        compiler_params=pltpu.CompilerParams(vmem_limit_bytes=4 << 20),
    )(first, a, pair)


def far_sums_kernel(mid_rows, _, a_ref, b_ref, pair_ref, *outs):
    for j, (x, o) in enumerate(zip((a_ref, b_ref), outs)):
        mid = pair_ref[j * mid_rows : (j + 1) * mid_rows].astype(jnp.float32)
        o[:mid_rows] = (x[:mid_rows].astype(jnp.float32) + mid).astype(jnp.bfloat16)
        root = root_of(x, mid_rows, None) + root_of(pair_ref, mid_rows, j)
        o[mid_rows:] = root.astype(jnp.bfloat16)


def far_sums(first, a, b, pair, mid_rows):
    return pl.pallas_call(
        functools.partial(far_sums_kernel, mid_rows),
        in_specs=[ANY] + [VMEM] * 3,
        out_shape=[jax.ShapeDtypeStruct(x.shape, x.dtype) for x in (a, b)],
        compiler_params=pltpu.CompilerParams(vmem_limit_bytes=8 << 20),
    )(*in_hbm(first), a, b, pair)


def mid_sums_kernel(mid_part, *refs):
    for i, o in enumerate(refs[-2:]):
        rows = slice(i * mid_part, (i + 1) * mid_part)
        total = refs[0][rows].astype(jnp.float32)
        for r in refs[1:-2]:
            total = total + r[rows].astype(jnp.float32)
        o[...] = total


def mid_sums(blocks, mid_part):
    return pl.pallas_call(
        functools.partial(mid_sums_kernel, mid_part),
        out_shape=[jax.ShapeDtypeStruct((mid_part, blocks[0].shape[1]), jnp.float32)] * 2,
        compiler_params=pltpu.CompilerParams(vmem_limit_bytes=8 << 20),
    )(*blocks)


def root_sums_kernel(count, mid_rows, root_own, paired, _, *refs):
    root = None
    for i, r in enumerate(refs[:count]):
        x = root_of(r, mid_rows, 0 if paired and i == 1 else None)
        root = x if root is None else root + x
    half = root.shape[0] // 2
    for t, o in enumerate(refs[count:]):
        o[:root_own] = root[t * root_own : (t + 1) * root_own]
        o[root_own:] = root[half + t * root_own : half + (t + 1) * root_own]


def root_sums(first, blocks, mid_rows, root_own, pieces):
    shape = jax.ShapeDtypeStruct((2 * root_own, blocks[0].shape[1]), jnp.float32)
    paired = blocks[1].shape[0] > blocks[0].shape[0]
    return pl.pallas_call(
        functools.partial(root_sums_kernel, len(blocks), mid_rows, root_own, paired),
        in_specs=[ANY] + [VMEM] * len(blocks),
        out_shape=[shape] * pieces,
        compiler_params=pltpu.CompilerParams(vmem_limit_bytes=8 << 20),
    )(*in_hbm(first), *blocks)


def root_kernel(root_own, *refs):
    total = refs[0][...]
    for r in refs[1:-2]:
        total = total + r[...]
    refs[-2][...] = total[:root_own]
    refs[-1][...] = total[root_own:]


def add_roots(pieces):
    rows, cols = pieces[0].shape
    return pl.pallas_call(
        functools.partial(root_kernel, rows // 2),
        out_shape=[jax.ShapeDtypeStruct((rows // 2, cols), jnp.float32)] * 2,
        compiler_params=pltpu.CompilerParams(vmem_limit_bytes=4 << 20),
    )(*pieces)


def swap(x, axis, size, offset):
    return lax.ppermute(x, axis, [(i, i ^ offset) for i in range(size)])


def on_device(
    mids,
    leaves,
    queries,
    out_grad,
    leaf_keys,
    leaf_values,
    mid_keys,
    mid_values,
    root_keys,
    root_values,
    mid_len,
    leaf_len,
):
    mid_part = mid_keys.shape[0]
    root_own = root_keys.shape[0]
    where = lax.axis_index("leaf").reshape(1).astype(jnp.int32)
    mid, pair = gather_own(mid_keys, mid_values, root_keys, root_values)
    mid_rows = 2 * mid_part
    same_core = range(2, mids, 2)
    pairs = [pair] + [swap(pair, "mid", mids, t) for t in same_core]
    block = pack((where, mid_len, leaf_len), mid, pairs)

    def leaf_swap(x, s):
        return swap(x, "leaf", leaves, s)

    far = [s for f in range(4, leaves, 4) for s in (f + 2, f)]
    far_blocks = {s: leaf_swap(block, s) for s in far}
    beside = leaf_swap(block, 1)
    operands = (queries, out_grad, leaf_keys, leaf_values)
    own = [own_part(0, block, *operands)]
    token = own[0][-1]
    blocks = [block, beside]
    if leaves >= 4:
        blocks.append(leaf_swap(join(token, block, beside, mid_rows), 2))
    for f in range(4, leaves, 4):
        x, y = far_blocks[f], far_blocks[f + 2]
        both = join(token, x, y, mid_rows)
        token = both
        blocks += [x, y, leaf_swap(both, 1)]
    own.append(own_part(1, token, *operands))
    root = collect(own[1][-1], blocks, leaves, mid_rows)
    roots = [root, swap(root, "mid", mids, 1)]
    keys, ds, own_p, mid_terms, root_terms = terms_part(
        where, mid_len, leaf_len, leaves, own, blocks, roots, mid_part
    )

    heads = leaf_keys.shape[1] // HD
    cuts = [0, heads // 4, heads]

    def query_part(first, i, so_far):
        return query_grads(first, cuts[i], cuts[i + 1] - cuts[i], so_far, queries, keys, ds)

    query_grad = query_part(where, 0, ())
    terms = spread(query_grad, root_terms[0], swap(root_terms[1], "mid", mids, 1), mid_terms)
    through = {f: leaf_swap(terms[3 * f // 4 + 2], 1) for f in range(4, leaves, 4)}
    query_grad = query_part(terms[0], 1, (query_grad,))
    near = leaf_swap(terms[2], 2) if leaves >= 4 else None
    arrived = [terms[0]] if near is None else [terms[0], near]
    last = terms[0]
    for f, x in through.items():
        n = 3 * f // 4
        a, last = far_sums(query_grad, terms[n], terms[n + 1], x, mid_rows)
        arrived += [leaf_swap(last, f + 2), leaf_swap(a, f)]
    beside = terms[1] if near is None else near_sum(last, terms[1], near, mid_rows)
    arrived.append(leaf_swap(beside, 1))
    leaf_key_grad, leaf_value_grad = own_grads(query_grad, queries, leaf_keys, own, own_p, ds)
    pieces = root_sums(leaf_value_grad, arrived, mid_rows, root_own, mids // 2)
    mid_key_grad, mid_value_grad = mid_sums(arrived, mid_part)
    pieces = [pieces[0]] + [swap(x, "mid", mids, t) for t, x in zip(same_core, pieces[1:])]
    root_key_grad, root_value_grad = add_roots(pieces)
    return (
        query_grad,
        leaf_key_grad,
        leaf_value_grad,
        mid_key_grad,
        mid_value_grad,
        root_key_grad,
        root_value_grad,
    )


def solution(mesh):
    both = P(("mid", "leaf"), None)
    in_specs = (both,) * 8 + (P("mid"), P(("mid", "leaf")))
    return jax.shard_map(
        functools.partial(on_device, mesh.shape["mid"], mesh.shape["leaf"]),
        mesh=mesh,
        in_specs=in_specs,
        out_specs=(both,) * 7,
        check_vma=False,
    )
```

```python
import functools
import math

import jax
import jax.numpy as jnp
from jax import lax
from jax.experimental import pallas as pl
from jax.experimental.pallas import tpu as pltpu
from jax.sharding import PartitionSpec as P

HD = 128
FACTOR = HD**-0.5
LOG2E = math.log2(math.e)
CHUNK = 16
NEG = -1e30
NT = (((1,), (1,)), ((), ()))
NN = (((1,), (0,)), ((), ()))
TN = (((0,), (0,)), ((), ()))


def dot(a, b, dims):
    return lax.dot_general(a, b, dims, preferred_element_type=jnp.float32)


def stacked(ref, part, half, heads_per):
    rows = slice(part * half, (part + 1) * half)
    return jnp.concatenate([ref[rows, h * HD : (h + 1) * HD] for h in range(heads_per)], 0)


def fold(x):
    return [x[i : i + 8] for i in range(0, x.shape[0], 8)]


def total_of(so_far, x, op):
    for y in fold(x):
        so_far = y if so_far is None else op(so_far, y)
    return so_far


def own_kernel(
    parity, _, q_hbm, g_hbm, k_hbm, v_hbm, q_ref, g_ref, k_ref, v_ref, e_ref, dp_ref, stats_ref, sems
):
    count, leaf_rows, span = q_ref.shape
    half = leaf_rows // 2
    heads_per = span // HD
    lanes = heads_per * half

    def copies(i):
        h = 2 * i + parity
        wide = pl.ds(pl.multiple_of(h * span, span), span)
        at = pl.ds(pl.multiple_of(h * HD, HD), HD)
        pairs = [
            (q_hbm.at[:, wide], q_ref.at[i]),
            (g_hbm.at[:, wide], g_ref.at[i]),
            (k_hbm.at[:, at], k_ref.at[i]),
            (v_hbm.at[:, at], v_ref.at[i]),
        ]
        return [pltpu.make_async_copy(x, y, sems.at[i, j]) for j, (x, y) in enumerate(pairs)]

    for i in range(count):
        for c in copies(i):
            c.start()
    chunk_row = lax.broadcasted_iota(jnp.int32, (CHUNK, half), 0)
    chunk_col = lax.broadcasted_iota(jnp.int32, (CHUNK, half), 1)

    @pl.loop(0, count)
    def one_head(i):
        for c in copies(i):
            c.wait()

        def scores(part):
            n, at = (part + 1) * half, part * half
            e_ref[i, at : at + n] = dot(k_ref[i, :n], stacked(q_ref.at[i], part, half, heads_per), NT)
            dp_ref[i, at : at + n] = dot(v_ref[i, :n], stacked(g_ref.at[i], part, half, heads_per), NT)

        def softmax(part):
            n, at = (part + 1) * half, part * half
            cols = slice(part * lanes, (part + 1) * lanes)

            def masked_chunk(r):
                s = e_ref[i, at + r : at + r + CHUNK]
                if r < n - half:
                    return s
                mask = chunk_row + (r - n + half) <= chunk_col
                return jnp.concatenate(
                    [jnp.where(mask, s[:, g * half : (g + 1) * half], NEG) for g in range(heads_per)], 1
                )

            starts = range(0, n, CHUNK)
            top = total = rd = None
            for r in starts:
                top = total_of(top, masked_chunk(r), jnp.maximum)
            top = jnp.max(top, axis=0, keepdims=True)
            for r in starts:
                e = jnp.exp2((masked_chunk(r) - top) * (FACTOR * LOG2E))
                e_ref[i, at + r : at + r + CHUNK] = e
                total = total_of(total, e, jnp.add)
                rd = total_of(rd, e * dp_ref[i, at + r : at + r + CHUNK], jnp.add)
            stats_ref[i, 0:1, cols] = top
            stats_ref[i, 1:2, cols] = jnp.sum(total, axis=0, keepdims=True)
            stats_ref[i, 2:3, cols] = jnp.sum(rd, axis=0, keepdims=True)

        scores(0)
        scores(1)
        softmax(0)
        softmax(1)


def places(slots, merged=True):
    if slots < 4:
        return [(s, None) for s in range(slots)]
    found = [(0, None), (1, None), (2, 0), (2, 1)]
    if not merged:
        return found + [(s - 1, None) for s in range(4, slots)]
    for n in range(3, 3 * slots // 4, 3):
        found += [(n, None), (n + 2, 0), (n + 1, None), (n + 2, 1)]
    return found


def arrays_of(slots):
    return max(i for i, _ in places(slots)) + 1


def terms_kernel(slots, mid_part, where_ref, mid_len_ref, leaf_len_ref, *refs):
    own_parts = refs[:7], refs[7:14]
    arrays = arrays_of(slots)
    block_refs = [
        refs[14 + i].at[pl.ds((j or 0) * 2 * mid_part, 2 * mid_part)] for i, j in places(slots)
    ]
    root_refs = refs[14 + arrays : 16 + arrays]
    outs = refs[16 + arrays :]
    keys_ref, ds_ref, own_p_ref = outs[:3]
    dmid_refs = outs[3 : 3 + slots]
    droot_refs = outs[3 + slots : 5 + slots]
    s_refs, dp_refs, p_refs = (outs[5 + slots + 2 * i : 7 + slots + 2 * i] for i in range(3))
    root_half = root_refs[0].shape[0] // 2
    me = where_ref[0]
    mid_live = mid_len_ref[0]
    leaf_live = leaf_len_ref[0]
    pairs, leaf_rows, span = own_parts[0][0].shape
    half = leaf_rows // 2
    heads_per = span // HD
    mid_rows = slots * mid_part
    root_rows = 2 * root_half
    shared = root_rows + mid_rows
    lanes = heads_per * half
    sizes = [shared + half, shared + 2 * half]
    chunk_row = lax.broadcasted_iota(jnp.int32, (CHUNK, half), 0)
    lane = lax.broadcasted_iota(jnp.int32, (1, half), 1)

    def live(part, x):
        alive = lane + part * half < leaf_live
        return jnp.concatenate(
            [jnp.where(alive, x[:, g * half : (g + 1) * half], 0.0) for g in range(heads_per)], 1
        )

    def masked_chunk(s_ref, r):
        s = s_ref[r : r + CHUNK]
        if r < root_rows:
            return s
        slot, rest = divmod(r - root_rows, mid_part)
        mask = chunk_row < mid_live - rest - jnp.bitwise_xor(me, slot) * mid_part
        return jnp.concatenate(
            [jnp.where(mask, s[:, g * half : (g + 1) * half], NEG) for g in range(heads_per)], 1
        )

    class Head:
        def __init__(self, i, parity):
            self.i = i
            self.h = h = 2 * i + parity
            self.at = pl.ds(pl.multiple_of(h * HD, HD), HD)
            q_ref, g_ref, k_ref, _, self.e_ref, self.own_dp_ref, self.stats_ref = own_parts[parity]
            self.keys = self.whole(0)
            self.values = self.whole(1)
            keys_ref[h, :shared] = self.keys
            keys_ref[h, shared:] = k_ref[i]
            self.qs = [stacked(q_ref.at[i], p, half, heads_per) for p in range(2)]
            self.gs = [stacked(g_ref.at[i], p, half, heads_per) for p in range(2)]
            self.dk, self.dv = [None, None], [None, None]

        def whole(self, which):
            at = self.at
            roots = [r[which * root_half : (which + 1) * root_half, at] for r in root_refs]
            mids = [r[which * mid_part : (which + 1) * mid_part, at] for r in block_refs]
            return jnp.concatenate(roots + mids, 0)

        def scores(self, part):
            s_refs[part][...] = dot(self.keys, self.qs[part], NT)
            dp_refs[part][...] = dot(self.values, self.gs[part], NT)

        def softmax(self, part):
            s_ref, dp_ref, p_ref = s_refs[part], dp_refs[part], p_refs[part]
            cols = slice(part * lanes, (part + 1) * lanes)
            own_top = self.stats_ref[self.i, 0:1, cols]
            top = total = rd = None
            starts = range(0, shared, CHUNK)
            for r in starts:
                top = total_of(top, masked_chunk(s_ref, r), jnp.maximum)
            top = jnp.maximum(jnp.max(top, axis=0, keepdims=True), own_top)
            own = jnp.exp2((own_top - top) * (FACTOR * LOG2E))
            for r in starts:
                e = jnp.exp2((masked_chunk(s_ref, r) - top) * (FACTOR * LOG2E))
                s_ref[r : r + CHUNK] = e
                total = total_of(total, e, jnp.add)
                rd = total_of(rd, e * dp_ref[r : r + CHUNK], jnp.add)
            total = jnp.sum(total, axis=0, keepdims=True) + own * self.stats_ref[self.i, 1:2, cols]
            inv = live(part, 1.0 / total)
            rd = jnp.sum(rd, axis=0, keepdims=True) + own * self.stats_ref[self.i, 2:3, cols]
            rd = rd * inv
            at = part * sizes[0]

            def finish(at, e, dp, scale, p_out, p_at):
                p = e * scale
                p_out[p_at : p_at + CHUNK] = p.astype(jnp.bfloat16)
                ds_ref[self.h, at : at + CHUNK] = (p * (dp - rd)).astype(jnp.bfloat16)

            for r in starts:
                finish(at + r, s_ref[r : r + CHUNK], dp_ref[r : r + CHUNK], inv, p_ref, r)
            own = own * inv
            for r in range(0, (part + 1) * half, CHUNK):
                to = part * half + r
                source = slice(to, to + CHUNK)
                e, dp = self.e_ref[self.i, source], self.own_dp_ref[self.i, source]
                finish(at + shared + r, e, dp, own, own_p_ref.at[self.h], to)

        def grads(self, part):
            at = part * sizes[0]
            self.dv[part] = dot(p_refs[part][...], self.gs[part], NN)
            self.dk[part] = dot(ds_ref[self.h, at : at + shared], self.qs[part], NN)

        def finish(self):
            dv = self.dv[0] + self.dv[1]
            dk = (self.dk[0] + self.dk[1]) * FACTOR
            at = self.at
            for i, o in enumerate(droot_refs):
                r = slice(i * root_half, (i + 1) * root_half)
                o[:, at] = jnp.concatenate([dk[r], dv[r]], 0).astype(jnp.bfloat16)
            for s, o in enumerate(dmid_refs):
                r = slice(root_rows + s * mid_part, root_rows + (s + 1) * mid_part)
                o[:, at] = jnp.concatenate([dk[r], dv[r]], 0).astype(jnp.bfloat16)

    @pl.loop(0, pairs)
    def two_heads(i):
        a, b = Head(i, 0), Head(i, 1)
        a.scores(0)
        a.scores(1)
        a.softmax(0)
        a.grads(0)
        b.scores(0)
        a.softmax(1)
        a.grads(1)
        b.scores(1)
        b.softmax(0)
        a.finish()
        b.grads(0)
        b.softmax(1)
        b.grads(1)
        b.finish()


def query_grads_kernel(heads_per, first, count, half, _, keys_ref, ds_ref, *refs):
    dq_hbm, dq_ref, sems = refs[-3:]
    n_all = keys_ref.shape[1]
    span = heads_per * HD

    def copy_out(i):
        at = pl.ds(pl.multiple_of(i * span, span), span)
        to = pl.ds(pl.multiple_of((i + first) * span, span), span)
        return pltpu.make_async_copy(dq_ref.at[:, at], dq_hbm.at[:, to], sems.at[i])

    @pl.loop(0, count)
    def one_head(i):
        keys = keys_ref[i + first]
        start = 0
        for part in range(2):
            n = n_all - (1 - part) * half
            dq = dot(keys[:n], ds_ref[i + first, start : start + n], TN)
            dq = (dq * FACTOR).T.astype(jnp.bfloat16)
            start += n
            for g in range(heads_per):
                at = pl.ds(pl.multiple_of(i * span + g * HD, HD), HD)
                dq_ref[part * half : (part + 1) * half, at] = dq[g * half : (g + 1) * half]
        copy_out(i).start()

    for i in range(count):
        copy_out(i).wait()


def own_grads_kernel(_, q0_ref, g0_ref, q1_ref, g1_ref, p_ref, ds_ref, dk_hbm, dv_hbm, dk_ref, dv_ref, sems):
    pairs, leaf_rows, span = q0_ref.shape
    half = leaf_rows // 2
    heads_per = span // HD
    first = ds_ref.shape[1] // 2 - half // 2

    def copies_out(h):
        at = pl.ds(pl.multiple_of(h * HD, HD), HD)
        return [
            pltpu.make_async_copy(x.at[:, at], y.at[:, at], sems.at[h, j])
            for j, (x, y) in enumerate(((dk_ref, dk_hbm), (dv_ref, dv_hbm)))
        ]

    @pl.loop(0, pairs)
    def two_heads(i):
        for parity, (q_ref, g_ref) in enumerate(((q0_ref, g0_ref), (q1_ref, g1_ref))):
            h = 2 * i + parity
            at = pl.ds(pl.multiple_of(h * HD, HD), HD)
            dk, dv = [], []
            for part in range(2):
                n = (part + 1) * half
                end = first if part == 0 else ds_ref.shape[1]
                qs = stacked(q_ref.at[i], part, half, heads_per)
                gs = stacked(g_ref.at[i], part, half, heads_per)
                dv.append(dot(p_ref[h, part * half : part * half + n], gs, NN))
                dk.append(dot(ds_ref[h, end - n : end], qs, NN))
            for x, ref, scale in ((dk, dk_ref, FACTOR), (dv, dv_ref, 1.0)):
                ref[:half, at] = ((x[0] + x[1][:half]) * scale).astype(jnp.bfloat16)
                ref[half:, at] = (x[1][half:] * scale).astype(jnp.bfloat16)
            for c in copies_out(h):
                c.start()

    for h in range(2 * pairs):
        for c in copies_out(h):
            c.wait()


def cost(matmuls, key_rows, queries, nbytes):
    rows, cols = queries.shape
    return pl.CostEstimate(
        flops=2 * matmuls * rows * key_rows * cols,
        bytes_accessed=nbytes,
        transcendentals=rows * key_rows * cols // HD,
    )


def in_hbm(*arrays):
    return [pltpu.with_memory_space_constraint(x, pltpu.HBM) for x in arrays]


ANY = pl.BlockSpec(memory_space=pl.ANY)
VMEM = pl.BlockSpec(memory_space=pltpu.VMEM)
SMEM = pl.BlockSpec(memory_space=pltpu.SMEM)


def own_part(parity, first, queries, out_grad, leaf_keys, leaf_values):
    rows, cols = leaf_keys.shape
    count = cols // (2 * HD)
    span = queries.shape[1] // cols * HD
    lanes = span // HD * rows // 2
    bf, f32 = jnp.bfloat16, jnp.float32
    shapes = [((rows, span), bf)] * 2 + [((rows, HD), bf)] * 2
    shapes += [((3 * rows // 2, lanes), f32)] * 2 + [((8, 2 * lanes), f32)]
    return pl.pallas_call(
        functools.partial(own_kernel, parity),
        in_specs=[ANY] * 5,
        out_specs=[VMEM] * len(shapes),
        out_shape=[jax.ShapeDtypeStruct((count,) + s, t) for s, t in shapes],
        scratch_shapes=[pltpu.SemaphoreType.DMA((count, 4))],
        compiler_params=pltpu.CompilerParams(vmem_limit_bytes=16 << 20),
        cost_estimate=cost(1, rows, queries, 2 * queries.size),
    )(first, *in_hbm(queries, out_grad, leaf_keys, leaf_values))


def terms_part(where, mid_len, leaf_len, slots, own, blocks, roots, mid_part):
    pairs, leaf_rows, span = own[0][0].shape
    cols = blocks[0].shape[1]
    heads = 2 * pairs
    shared = slots * mid_part + roots[0].shape[0]
    key_rows = shared + leaf_rows
    half = leaf_rows // 2
    lanes = span // HD * half
    bf, f32 = jnp.bfloat16, jnp.float32
    shapes = [
        (heads, key_rows, HD),
        (heads, 2 * key_rows - half, lanes),
        (heads, 3 * half, lanes),
    ]
    shapes += [(2 * mid_part, cols)] * slots + [x.shape for x in roots]
    out = pl.pallas_call(
        functools.partial(terms_kernel, slots, mid_part),
        in_specs=[SMEM] * 3 + [VMEM] * (16 + len(blocks)),
        out_specs=[VMEM] * len(shapes),
        out_shape=[jax.ShapeDtypeStruct(s, bf) for s in shapes],
        scratch_shapes=[pltpu.VMEM((shared, lanes), f32) for _ in range(4)]
        + [pltpu.VMEM((shared, lanes), bf) for _ in range(2)],
        compiler_params=pltpu.CompilerParams(vmem_limit_bytes=(14 if shared <= 256 else 52) << 20),
        cost_estimate=pl.CostEstimate(
            flops=8 * leaf_rows * key_rows * span * heads,
            bytes_accessed=4 * leaf_rows * span * heads,
            transcendentals=leaf_rows * key_rows * heads,
        ),
    )(where, mid_len, leaf_len, *own[0], *own[1], *blocks, *roots)
    return out[0], out[1], out[2], out[3 : 3 + slots], out[3 + slots :]


def query_grads(after_this, first, count, so_far, queries, keys, ds):
    rows, cols = queries.shape
    heads = keys.shape[0]
    heads_per = cols // (heads * HD)
    return pl.pallas_call(
        functools.partial(query_grads_kernel, heads_per, first, count, rows // 2),
        in_specs=[ANY] + [VMEM] * 2 + [ANY] * len(so_far),
        out_specs=ANY,
        out_shape=jax.ShapeDtypeStruct(queries.shape, jnp.bfloat16),
        input_output_aliases={3 + i: i for i in range(len(so_far))},
        scratch_shapes=[
            pltpu.VMEM((rows, count * heads_per * HD), jnp.bfloat16),
            pltpu.SemaphoreType.DMA((count,)),
        ],
        compiler_params=pltpu.CompilerParams(
            vmem_limit_bytes=(10 if keys.shape[1] <= 512 else 32) << 20
        ),
        cost_estimate=cost(1, keys.shape[1] * count // heads, queries, 2 * queries.size),
    )(after_this, keys, ds, *so_far)


def last_grads_kernel(heads_per, first, count, half, after_ref, keys_ref, ds_ref, q0, g0, q1, g1, p_ref, *refs):
    dq_hbm, dk_hbm, dv_hbm, dq_ref, dk_ref, dv_ref, dq_sems, own_sems = refs[1:]
    query_grads_kernel(heads_per, first, count, half, after_ref, keys_ref, ds_ref, dq_hbm, dq_ref, dq_sems)
    own_grads_kernel(after_ref, q0, g0, q1, g1, p_ref, ds_ref, dk_hbm, dv_hbm, dk_ref, dv_ref, own_sems)


def last_grads(after_this, first, so_far, leaf_keys, own, keys, p, ds):
    rows, cols = so_far.shape
    heads = keys.shape[0]
    count = heads - first
    span = cols // heads
    own_shape = jax.ShapeDtypeStruct(leaf_keys.shape, jnp.bfloat16)
    return pl.pallas_call(
        functools.partial(last_grads_kernel, span // HD, first, count, rows // 2),
        in_specs=[ANY] + [VMEM] * 7 + [ANY],
        out_specs=[ANY] * 3,
        out_shape=[jax.ShapeDtypeStruct(so_far.shape, jnp.bfloat16), own_shape, own_shape],
        input_output_aliases={8: 0},
        scratch_shapes=[pltpu.VMEM((rows, count * span), jnp.bfloat16)]
        + [pltpu.VMEM(own_shape.shape, jnp.bfloat16)] * 2
        + [pltpu.SemaphoreType.DMA(s) for s in ((count,), (heads, 2))],
        compiler_params=pltpu.CompilerParams(
            vmem_limit_bytes=(10 if ds.shape[1] <= 1024 else 52) << 20
        ),
        cost_estimate=cost(2, keys.shape[1], so_far, 2 * so_far.size),
    )(after_this, keys, ds, *own[0][:2], *own[1][:2], p, so_far)


def gather_kernel(mk_ref, mv_ref, rk_ref, rv_ref, mid_ref, pair_ref):
    mid_ref[...] = jnp.concatenate([mk_ref[...], mv_ref[...]], 0)
    pair_ref[...] = jnp.concatenate([rk_ref[...], rv_ref[...]], 0)


def gather_own(mid_keys, mid_values, root_keys, root_values):
    return pl.pallas_call(
        gather_kernel,
        out_shape=[
            jax.ShapeDtypeStruct((2 * x.shape[0], x.shape[1]), x.dtype)
            for x in (mid_keys, root_keys)
        ],
        compiler_params=pltpu.CompilerParams(vmem_limit_bytes=4 << 20),
    )(*in_hbm(mid_keys, mid_values, root_keys, root_values))


def pack_kernel(root_own, where_ref, mid_len_ref, leaf_len_ref, mid_ref, *refs):
    pairs = [r[...].astype(jnp.float32) for r in refs[:-1]]
    roots = [p[:root_own] for p in pairs] + [p[root_own:] for p in pairs]
    refs[-1][...] = jnp.concatenate(
        [mid_ref[...], jnp.concatenate(roots, 0).astype(jnp.bfloat16)], 0
    )


def pack(scalars, mid, pairs):
    rows = mid.shape[0] + len(pairs) * pairs[0].shape[0]
    return pl.pallas_call(
        functools.partial(pack_kernel, pairs[0].shape[0] // 2),
        in_specs=[SMEM] * 3 + [VMEM] * (1 + len(pairs)),
        out_shape=jax.ShapeDtypeStruct((rows, mid.shape[1]), jnp.bfloat16),
        compiler_params=pltpu.CompilerParams(vmem_limit_bytes=4 << 20),
    )(*scalars, mid, *pairs)


def join_kernel(mid_rows, _, a_ref, b_ref, out_ref):
    rows = a_ref.shape[0]
    out_ref[:mid_rows] = a_ref[:mid_rows]
    out_ref[mid_rows : 2 * mid_rows] = b_ref[:mid_rows]
    roots = [r[mid_rows:rows].astype(jnp.float32) for r in (a_ref, b_ref)]
    out_ref[2 * mid_rows :] = jnp.concatenate(roots, 0).astype(jnp.bfloat16)


def join(first, a, b, mid_rows):
    return pl.pallas_call(
        functools.partial(join_kernel, mid_rows),
        out_shape=jax.ShapeDtypeStruct((2 * a.shape[0], a.shape[1]), a.dtype),
        compiler_params=pltpu.CompilerParams(vmem_limit_bytes=4 << 20),
    )(first, a, b)


def root_of(ref, mid_rows, place):
    if place is None:
        return ref[mid_rows:].astype(jnp.float32)
    both = ref[2 * mid_rows :].astype(jnp.float32)
    rows = both.shape[0] // 2
    return both[place * rows : (place + 1) * rows]


def collect_kernel(slots, mid_rows, _, *refs):
    out_ref = refs[-1]
    roots = [root_of(refs[i], mid_rows, j) for i, j in places(slots)]
    half = roots[0].shape[0] // 2
    out_ref[...] = jnp.concatenate(
        [r[:half] for r in roots] + [r[half:] for r in roots], 0
    ).astype(jnp.bfloat16)


def collect(first, blocks, slots, mid_rows):
    rows = slots * (blocks[0].shape[0] - mid_rows)
    return pl.pallas_call(
        functools.partial(collect_kernel, slots, mid_rows),
        in_specs=[ANY] + [VMEM] * len(blocks),
        out_shape=jax.ShapeDtypeStruct((rows, blocks[0].shape[1]), jnp.bfloat16),
        compiler_params=pltpu.CompilerParams(vmem_limit_bytes=8 << 20),
    )(first, *blocks)


def spread_kernel(slots, mid_rows, _, a_ref, b_ref, *refs):
    mids, outs = refs[:slots], refs[slots:]
    total = a_ref[...].astype(jnp.float32) + b_ref[...].astype(jnp.float32)
    half = total.shape[0] // 2
    part = half // slots
    roots = [
        jnp.concatenate([total[at + s * part : at + (s + 1) * part] for at in (0, half)], 0)
        for s in range(slots)
    ]
    held = {}
    for s, (i, j) in enumerate(places(slots, False)):
        at = mid_rows * (j or 0)
        outs[i][at : at + mid_rows] = mids[s][...]
        held.setdefault(i, []).append(roots[s])
    for i, x in held.items():
        outs[i][len(x) * mid_rows :] = jnp.concatenate(x, 0).astype(jnp.bfloat16)


def spread(first, a, b, mids):
    slots = len(mids)
    mid_rows, cols = mids[0].shape
    rows = mid_rows + a.shape[0] // slots
    found = places(slots, False)
    paired = {i for i, j in found if j is not None}
    shapes = [(2 * rows if i in paired else rows, cols) for i in range(found[-1][0] + 1)]
    return pl.pallas_call(
        functools.partial(spread_kernel, slots, mid_rows),
        in_specs=[ANY] + [VMEM] * (2 + slots),
        out_shape=[jax.ShapeDtypeStruct(x, jnp.bfloat16) for x in shapes],
        compiler_params=pltpu.CompilerParams(vmem_limit_bytes=8 << 20),
    )(*in_hbm(first), a, b, *mids)


def near_sum_kernel(mid_rows, _, a_ref, pair_ref, out_ref):
    pair = pair_ref[mid_rows : 2 * mid_rows].astype(jnp.float32)
    out_ref[:mid_rows] = (a_ref[:mid_rows].astype(jnp.float32) + pair).astype(jnp.bfloat16)
    root = root_of(a_ref, mid_rows, None) + root_of(pair_ref, mid_rows, 1)
    out_ref[mid_rows:] = root.astype(jnp.bfloat16)


def near_sum(first, a, pair, mid_rows):
    return pl.pallas_call(
        functools.partial(near_sum_kernel, mid_rows),
        in_specs=[ANY] + [VMEM] * 2,
        out_shape=jax.ShapeDtypeStruct(a.shape, a.dtype),
        compiler_params=pltpu.CompilerParams(vmem_limit_bytes=4 << 20),
    )(first, a, pair)


def far_sum_kernel(_, a_ref, b_ref, out_ref):
    out_ref[...] = (a_ref[...].astype(jnp.float32) + b_ref[...].astype(jnp.float32)).astype(jnp.bfloat16)


def far_sum(first, a, b):
    return pl.pallas_call(
        far_sum_kernel,
        in_specs=[ANY] + [VMEM] * 2,
        out_shape=jax.ShapeDtypeStruct(a.shape, a.dtype),
        compiler_params=pltpu.CompilerParams(vmem_limit_bytes=4 << 20),
    )(first, a, b)


def mid_sums_kernel(mid_part, *refs):
    for i, o in enumerate(refs[-2:]):
        rows = slice(i * mid_part, (i + 1) * mid_part)
        total = refs[0][rows].astype(jnp.float32)
        for r in refs[1:-2]:
            total = total + r[rows].astype(jnp.float32)
        o[...] = total


def mid_sums(blocks, mid_part):
    return pl.pallas_call(
        functools.partial(mid_sums_kernel, mid_part),
        out_shape=[jax.ShapeDtypeStruct((mid_part, blocks[0].shape[1]), jnp.float32)] * 2,
        compiler_params=pltpu.CompilerParams(vmem_limit_bytes=8 << 20),
    )(*blocks)


def root_sums_kernel(count, mid_rows, root_own, paired, _, *refs):
    root = None
    for i, r in enumerate(refs[:count]):
        x = root_of(r, mid_rows, 0 if paired and i == 1 else None)
        root = x if root is None else root + x
    half = root.shape[0] // 2
    for t, o in enumerate(refs[count:]):
        o[:root_own] = root[t * root_own : (t + 1) * root_own]
        o[root_own:] = root[half + t * root_own : half + (t + 1) * root_own]


def root_sums(first, blocks, mid_rows, root_own, pieces):
    shape = jax.ShapeDtypeStruct((2 * root_own, blocks[0].shape[1]), jnp.float32)
    paired = blocks[1].shape[0] > blocks[0].shape[0]
    return pl.pallas_call(
        functools.partial(root_sums_kernel, len(blocks), mid_rows, root_own, paired),
        in_specs=[ANY] + [VMEM] * len(blocks),
        out_shape=[shape] * pieces,
        compiler_params=pltpu.CompilerParams(vmem_limit_bytes=8 << 20),
    )(*in_hbm(first), *blocks)


def root_kernel(root_own, *refs):
    total = refs[0][...]
    for r in refs[1:-2]:
        total = total + r[...]
    refs[-2][...] = total[:root_own]
    refs[-1][...] = total[root_own:]


def add_roots(pieces):
    rows, cols = pieces[0].shape
    return pl.pallas_call(
        functools.partial(root_kernel, rows // 2),
        out_shape=[jax.ShapeDtypeStruct((rows // 2, cols), jnp.float32)] * 2,
        compiler_params=pltpu.CompilerParams(vmem_limit_bytes=4 << 20),
    )(*pieces)


def swap(x, axis, size, offset):
    return lax.ppermute(x, axis, [(i, i ^ offset) for i in range(size)])


def on_device(
    mids,
    leaves,
    queries,
    out_grad,
    leaf_keys,
    leaf_values,
    mid_keys,
    mid_values,
    root_keys,
    root_values,
    mid_len,
    leaf_len,
):
    mid_part = mid_keys.shape[0]
    root_own = root_keys.shape[0]
    where = lax.axis_index("leaf").reshape(1).astype(jnp.int32)
    mid, pair = gather_own(mid_keys, mid_values, root_keys, root_values)
    mid_rows = 2 * mid_part
    same_core = range(2, mids, 2)
    pairs = [pair] + [swap(pair, "mid", mids, t) for t in same_core]
    block = pack((where, mid_len, leaf_len), mid, pairs)

    def leaf_swap(x, s):
        return swap(x, "leaf", leaves, s)

    far = [s for f in range(4, leaves, 4) for s in (f + 2, f)]
    far_blocks = {s: leaf_swap(block, s) for s in far}
    beside = leaf_swap(block, 1)
    operands = (queries, out_grad, leaf_keys, leaf_values)
    own = [own_part(0, block, *operands)]
    token = own[0][-1]
    blocks = [block, beside]
    if leaves >= 4:
        blocks.append(leaf_swap(join(token, block, beside, mid_rows), 2))
    for f in range(4, leaves, 4):
        x, y = far_blocks[f], far_blocks[f + 2]
        both = join(token, x, y, mid_rows)
        token = both
        blocks += [x, y, leaf_swap(both, 1)]
    own.append(own_part(1, token, *operands))
    root = collect(own[1][-1], blocks, leaves, mid_rows)
    roots = [root, swap(root, "mid", mids, 1)]
    keys, ds, own_p, mid_terms, root_terms = terms_part(
        where, mid_len, leaf_len, leaves, own, blocks, roots, mid_part
    )

    heads = leaf_keys.shape[1] // HD
    cuts = [0, heads // 4, heads // 2, heads]

    def query_part(first, i, so_far):
        return query_grads(first, cuts[i], cuts[i + 1] - cuts[i], so_far, queries, keys, ds)

    query_grad = query_part(where, 0, ())
    terms = spread(query_grad, root_terms[0], swap(root_terms[1], "mid", mids, 1), mid_terms)
    through = [leaf_swap(terms[s], 1) for s in far]
    query_grad = query_part(terms[0], 1, (query_grad,))
    (token,) = in_hbm(query_grad)
    near = leaf_swap(terms[2], 2) if leaves >= 4 else None
    arrived = [terms[0]] if near is None else [terms[0], near]
    last = terms[0]
    for s, x in zip(far, through):
        last = far_sum(token, terms[s - 1], x)
        token = last
        arrived.append(leaf_swap(last, s))
    beside = terms[1] if near is None else near_sum(last, terms[1], near, mid_rows)
    arrived.append(leaf_swap(beside, 1))
    query_grad, leaf_key_grad, leaf_value_grad = last_grads(
        beside, cuts[2], query_grad, leaf_keys, own, keys, own_p, ds
    )
    pieces = root_sums(leaf_value_grad, arrived, mid_rows, root_own, mids // 2)
    mid_key_grad, mid_value_grad = mid_sums(arrived, mid_part)
    pieces = [pieces[0]] + [swap(x, "mid", mids, t) for t, x in zip(same_core, pieces[1:])]
    root_key_grad, root_value_grad = add_roots(pieces)
    return (
        query_grad,
        leaf_key_grad,
        leaf_value_grad,
        mid_key_grad,
        mid_value_grad,
        root_key_grad,
        root_value_grad,
    )


def solution(mesh):
    both = P(("mid", "leaf"), None)
    in_specs = (both,) * 8 + (P("mid"), P(("mid", "leaf")))
    return jax.shard_map(
        functools.partial(on_device, mesh.shape["mid"], mesh.shape["leaf"]),
        mesh=mesh,
        in_specs=in_specs,
        out_specs=(both,) * 7,
        check_vma=False,
    )
```

```python
import functools
import math

import jax
import jax.numpy as jnp
from jax import lax
from jax.experimental import pallas as pl
from jax.experimental.pallas import tpu as pltpu
from jax.sharding import PartitionSpec as P

HD = 128
FACTOR = HD**-0.5
LOG2E = math.log2(math.e)
CHUNK = 16
NEG = -1e30
NT = (((1,), (1,)), ((), ()))
NN = (((1,), (0,)), ((), ()))
TN = (((0,), (0,)), ((), ()))


def dot(a, b, dims):
    return lax.dot_general(a, b, dims, preferred_element_type=jnp.float32)


def stacked(ref, part, half, heads_per):
    rows = slice(part * half, (part + 1) * half)
    return jnp.concatenate([ref[rows, h * HD : (h + 1) * HD] for h in range(heads_per)], 0)


def fold(x):
    return [x[i : i + 8] for i in range(0, x.shape[0], 8)]


def total_of(so_far, x, op):
    for y in fold(x):
        so_far = y if so_far is None else op(so_far, y)
    return so_far


def own_kernel(
    parity, _, q_hbm, g_hbm, k_hbm, v_hbm, q_ref, g_ref, k_ref, v_ref, e_ref, dp_ref, stats_ref, sems
):
    count, leaf_rows, span = q_ref.shape
    half = leaf_rows // 2
    heads_per = span // HD
    lanes = heads_per * half

    def copies(i):
        h = 2 * i + parity
        wide = pl.ds(pl.multiple_of(h * span, span), span)
        at = pl.ds(pl.multiple_of(h * HD, HD), HD)
        pairs = [
            (q_hbm.at[:, wide], q_ref.at[i]),
            (g_hbm.at[:, wide], g_ref.at[i]),
            (k_hbm.at[:, at], k_ref.at[i]),
            (v_hbm.at[:, at], v_ref.at[i]),
        ]
        return [pltpu.make_async_copy(x, y, sems.at[i, j]) for j, (x, y) in enumerate(pairs)]

    for i in range(count):
        for c in copies(i):
            c.start()
    chunk_row = lax.broadcasted_iota(jnp.int32, (CHUNK, half), 0)
    chunk_col = lax.broadcasted_iota(jnp.int32, (CHUNK, half), 1)

    @pl.loop(0, count)
    def one_head(i):
        for c in copies(i):
            c.wait()

        def scores(part):
            n, at = (part + 1) * half, part * half
            e_ref[i, at : at + n] = dot(k_ref[i, :n], stacked(q_ref.at[i], part, half, heads_per), NT)
            dp_ref[i, at : at + n] = dot(v_ref[i, :n], stacked(g_ref.at[i], part, half, heads_per), NT)

        def softmax(part):
            n, at = (part + 1) * half, part * half
            cols = slice(part * lanes, (part + 1) * lanes)

            def masked_chunk(r):
                s = e_ref[i, at + r : at + r + CHUNK]
                if r < n - half:
                    return s
                mask = chunk_row + (r - n + half) <= chunk_col
                return jnp.concatenate(
                    [jnp.where(mask, s[:, g * half : (g + 1) * half], NEG) for g in range(heads_per)], 1
                )

            starts = range(0, n, CHUNK)
            top = total = rd = None
            for r in starts:
                top = total_of(top, masked_chunk(r), jnp.maximum)
            top = jnp.max(top, axis=0, keepdims=True)
            for r in starts:
                e = jnp.exp2((masked_chunk(r) - top) * (FACTOR * LOG2E))
                e_ref[i, at + r : at + r + CHUNK] = e
                total = total_of(total, e, jnp.add)
                rd = total_of(rd, e * dp_ref[i, at + r : at + r + CHUNK], jnp.add)
            stats_ref[i, 0:1, cols] = top
            stats_ref[i, 1:2, cols] = jnp.sum(total, axis=0, keepdims=True)
            stats_ref[i, 2:3, cols] = jnp.sum(rd, axis=0, keepdims=True)

        scores(0)
        scores(1)
        softmax(0)
        softmax(1)


def places(slots, merged=True):
    if slots < 4:
        return [(s, None) for s in range(slots)]
    found = [(0, None), (1, None), (2, 0), (2, 1)]
    if not merged:
        return found + [(s - 1, None) for s in range(4, slots)]
    for n in range(3, 3 * slots // 4, 3):
        found += [(n, None), (n + 2, 0), (n + 1, None), (n + 2, 1)]
    return found


def arrays_of(slots):
    return max(i for i, _ in places(slots)) + 1


def terms_kernel(slots, mid_part, where_ref, mid_len_ref, leaf_len_ref, *refs):
    own_parts = refs[:7], refs[7:14]
    arrays = arrays_of(slots)
    block_refs = [
        refs[14 + i].at[pl.ds((j or 0) * 2 * mid_part, 2 * mid_part)] for i, j in places(slots)
    ]
    root_refs = refs[14 + arrays : 16 + arrays]
    outs = refs[16 + arrays :]
    keys_ref, ds_ref, own_p_ref = outs[:3]
    dmid_refs = outs[3 : 3 + slots]
    droot_refs = outs[3 + slots : 5 + slots]
    s_refs, dp_refs, p_refs = (outs[5 + slots + 2 * i : 7 + slots + 2 * i] for i in range(3))
    root_half = root_refs[0].shape[0] // 2
    me = where_ref[0]
    mid_live = mid_len_ref[0]
    leaf_live = leaf_len_ref[0]
    pairs, leaf_rows, span = own_parts[0][0].shape
    half = leaf_rows // 2
    heads_per = span // HD
    mid_rows = slots * mid_part
    root_rows = 2 * root_half
    shared = root_rows + mid_rows
    lanes = heads_per * half
    sizes = [shared + half, shared + 2 * half]
    chunk_row = lax.broadcasted_iota(jnp.int32, (CHUNK, half), 0)
    lane = lax.broadcasted_iota(jnp.int32, (1, half), 1)

    def live(part, x):
        alive = lane + part * half < leaf_live
        return jnp.concatenate(
            [jnp.where(alive, x[:, g * half : (g + 1) * half], 0.0) for g in range(heads_per)], 1
        )

    def masked_chunk(s_ref, r):
        s = s_ref[r : r + CHUNK]
        if r < root_rows:
            return s
        slot, rest = divmod(r - root_rows, mid_part)
        mask = chunk_row < mid_live - rest - jnp.bitwise_xor(me, slot) * mid_part
        return jnp.concatenate(
            [jnp.where(mask, s[:, g * half : (g + 1) * half], NEG) for g in range(heads_per)], 1
        )

    class Head:
        def __init__(self, i, parity):
            self.i = i
            self.h = h = 2 * i + parity
            self.at = pl.ds(pl.multiple_of(h * HD, HD), HD)
            q_ref, g_ref, k_ref, _, self.e_ref, self.own_dp_ref, self.stats_ref = own_parts[parity]
            self.keys = self.whole(0)
            self.values = self.whole(1)
            keys_ref[h, :shared] = self.keys
            keys_ref[h, shared:] = k_ref[i]
            self.qs = [stacked(q_ref.at[i], p, half, heads_per) for p in range(2)]
            self.gs = [stacked(g_ref.at[i], p, half, heads_per) for p in range(2)]
            self.dk, self.dv = [None, None], [None, None]

        def whole(self, which):
            at = self.at
            roots = [r[which * root_half : (which + 1) * root_half, at] for r in root_refs]
            mids = [r[which * mid_part : (which + 1) * mid_part, at] for r in block_refs]
            return jnp.concatenate(roots + mids, 0)

        def scores(self, part):
            s_refs[part][...] = dot(self.keys, self.qs[part], NT)
            dp_refs[part][...] = dot(self.values, self.gs[part], NT)

        def softmax(self, part):
            s_ref, dp_ref, p_ref = s_refs[part], dp_refs[part], p_refs[part]
            cols = slice(part * lanes, (part + 1) * lanes)
            own_top = self.stats_ref[self.i, 0:1, cols]
            top = total = rd = None
            starts = range(0, shared, CHUNK)
            for r in starts:
                top = total_of(top, masked_chunk(s_ref, r), jnp.maximum)
            top = jnp.maximum(jnp.max(top, axis=0, keepdims=True), own_top)
            own = jnp.exp2((own_top - top) * (FACTOR * LOG2E))
            for r in starts:
                e = jnp.exp2((masked_chunk(s_ref, r) - top) * (FACTOR * LOG2E))
                s_ref[r : r + CHUNK] = e
                total = total_of(total, e, jnp.add)
                rd = total_of(rd, e * dp_ref[r : r + CHUNK], jnp.add)
            total = jnp.sum(total, axis=0, keepdims=True) + own * self.stats_ref[self.i, 1:2, cols]
            inv = live(part, 1.0 / total)
            rd = jnp.sum(rd, axis=0, keepdims=True) + own * self.stats_ref[self.i, 2:3, cols]
            rd = rd * inv
            at = part * sizes[0]

            def finish(at, e, dp, scale, p_out, p_at):
                p = e * scale
                p_out[p_at : p_at + CHUNK] = p.astype(jnp.bfloat16)
                ds_ref[self.h, at : at + CHUNK] = (p * (dp - rd)).astype(jnp.bfloat16)

            for r in starts:
                finish(at + r, s_ref[r : r + CHUNK], dp_ref[r : r + CHUNK], inv, p_ref, r)
            own = own * inv
            for r in range(0, (part + 1) * half, CHUNK):
                to = part * half + r
                source = slice(to, to + CHUNK)
                e, dp = self.e_ref[self.i, source], self.own_dp_ref[self.i, source]
                finish(at + shared + r, e, dp, own, own_p_ref.at[self.h], to)

        def grads(self, part):
            at = part * sizes[0]
            self.dv[part] = dot(p_refs[part][...], self.gs[part], NN)
            self.dk[part] = dot(ds_ref[self.h, at : at + shared], self.qs[part], NN)

        def finish(self):
            dv = self.dv[0] + self.dv[1]
            dk = (self.dk[0] + self.dk[1]) * FACTOR
            at = self.at
            for i, o in enumerate(droot_refs):
                r = slice(i * root_half, (i + 1) * root_half)
                o[:, at] = jnp.concatenate([dk[r], dv[r]], 0).astype(jnp.bfloat16)
            for s, o in enumerate(dmid_refs):
                r = slice(root_rows + s * mid_part, root_rows + (s + 1) * mid_part)
                o[:, at] = jnp.concatenate([dk[r], dv[r]], 0).astype(jnp.bfloat16)

    @pl.loop(0, pairs)
    def two_heads(i):
        a, b = Head(i, 0), Head(i, 1)
        a.scores(0)
        a.scores(1)
        a.softmax(0)
        a.grads(0)
        b.scores(0)
        a.softmax(1)
        a.grads(1)
        b.scores(1)
        b.softmax(0)
        a.finish()
        b.grads(0)
        b.softmax(1)
        b.grads(1)
        b.finish()


def query_grads_kernel(heads_per, first, count, half, finish, _, keys_ref, ds_ref, *refs):
    dq_hbm, dq_ref, sems = refs[-3:]
    n_all = keys_ref.shape[1]
    span = heads_per * HD

    def copy_out(i):
        at = pl.ds(pl.multiple_of(i * span, span), span)
        to = pl.ds(pl.multiple_of((i + first) * span, span), span)
        return pltpu.make_async_copy(dq_ref.at[:, at], dq_hbm.at[:, to], sems.at[i])

    @pl.loop(0, count)
    def one_head(i):
        keys = keys_ref[i + first]
        start = 0
        for part in range(2):
            n = n_all - (1 - part) * half
            dq = dot(keys[:n], ds_ref[i + first, start : start + n], TN)
            dq = (dq * FACTOR).T.astype(jnp.bfloat16)
            start += n
            for g in range(heads_per):
                at = pl.ds(pl.multiple_of(i * span + g * HD, HD), HD)
                dq_ref[part * half : (part + 1) * half, at] = dq[g * half : (g + 1) * half]
        copy_out(i).start()

    def wait():
        for i in range(count):
            copy_out(i).wait()

    if finish:
        wait()
    return wait


def run_query_grads(heads_per, first, count, half, *refs):
    query_grads_kernel(heads_per, first, count, half, True, *refs)


def own_grads_kernel(_, q0_ref, g0_ref, q1_ref, g1_ref, p_ref, ds_ref, dk_hbm, dv_hbm, dk_ref, dv_ref, sems):
    pairs, leaf_rows, span = q0_ref.shape
    half = leaf_rows // 2
    heads_per = span // HD
    first = ds_ref.shape[1] // 2 - half // 2

    def copies_out(h):
        at = pl.ds(pl.multiple_of(h * HD, HD), HD)
        return [
            pltpu.make_async_copy(x.at[:, at], y.at[:, at], sems.at[h, j])
            for j, (x, y) in enumerate(((dk_ref, dk_hbm), (dv_ref, dv_hbm)))
        ]

    @pl.loop(0, pairs)
    def two_heads(i):
        for parity, (q_ref, g_ref) in enumerate(((q0_ref, g0_ref), (q1_ref, g1_ref))):
            h = 2 * i + parity
            at = pl.ds(pl.multiple_of(h * HD, HD), HD)
            dk, dv = [], []
            for part in range(2):
                n = (part + 1) * half
                end = first if part == 0 else ds_ref.shape[1]
                qs = stacked(q_ref.at[i], part, half, heads_per)
                gs = stacked(g_ref.at[i], part, half, heads_per)
                dv.append(dot(p_ref[h, part * half : part * half + n], gs, NN))
                dk.append(dot(ds_ref[h, end - n : end], qs, NN))
            for x, ref, scale in ((dk, dk_ref, FACTOR), (dv, dv_ref, 1.0)):
                ref[:half, at] = ((x[0] + x[1][:half]) * scale).astype(jnp.bfloat16)
                ref[half:, at] = (x[1][half:] * scale).astype(jnp.bfloat16)
            for c in copies_out(h):
                c.start()

    for h in range(2 * pairs):
        for c in copies_out(h):
            c.wait()


def cost(matmuls, key_rows, queries, nbytes):
    rows, cols = queries.shape
    return pl.CostEstimate(
        flops=2 * matmuls * rows * key_rows * cols,
        bytes_accessed=nbytes,
        transcendentals=rows * key_rows * cols // HD,
    )


def in_hbm(*arrays):
    return [pltpu.with_memory_space_constraint(x, pltpu.HBM) for x in arrays]


ANY = pl.BlockSpec(memory_space=pl.ANY)
VMEM = pl.BlockSpec(memory_space=pltpu.VMEM)
SMEM = pl.BlockSpec(memory_space=pltpu.SMEM)


def own_part(parity, first, queries, out_grad, leaf_keys, leaf_values):
    rows, cols = leaf_keys.shape
    count = cols // (2 * HD)
    span = queries.shape[1] // cols * HD
    lanes = span // HD * rows // 2
    bf, f32 = jnp.bfloat16, jnp.float32
    shapes = [((rows, span), bf)] * 2 + [((rows, HD), bf)] * 2
    shapes += [((3 * rows // 2, lanes), f32)] * 2 + [((8, 2 * lanes), f32)]
    return pl.pallas_call(
        functools.partial(own_kernel, parity),
        in_specs=[ANY] * 5,
        out_specs=[VMEM] * len(shapes),
        out_shape=[jax.ShapeDtypeStruct((count,) + s, t) for s, t in shapes],
        scratch_shapes=[pltpu.SemaphoreType.DMA((count, 4))],
        compiler_params=pltpu.CompilerParams(vmem_limit_bytes=16 << 20),
        cost_estimate=cost(1, rows, queries, 2 * queries.size),
    )(first, *in_hbm(queries, out_grad, leaf_keys, leaf_values))


def terms_part(where, mid_len, leaf_len, slots, own, blocks, roots, mid_part):
    pairs, leaf_rows, span = own[0][0].shape
    cols = blocks[0].shape[1]
    heads = 2 * pairs
    shared = slots * mid_part + roots[0].shape[0]
    key_rows = shared + leaf_rows
    half = leaf_rows // 2
    lanes = span // HD * half
    bf, f32 = jnp.bfloat16, jnp.float32
    shapes = [
        (heads, key_rows, HD),
        (heads, 2 * key_rows - half, lanes),
        (heads, 3 * half, lanes),
    ]
    shapes += [(2 * mid_part, cols)] * slots + [x.shape for x in roots]
    out = pl.pallas_call(
        functools.partial(terms_kernel, slots, mid_part),
        in_specs=[SMEM] * 3 + [VMEM] * (16 + len(blocks)),
        out_specs=[VMEM] * len(shapes),
        out_shape=[jax.ShapeDtypeStruct(s, bf) for s in shapes],
        scratch_shapes=[pltpu.VMEM((shared, lanes), f32) for _ in range(4)]
        + [pltpu.VMEM((shared, lanes), bf) for _ in range(2)],
        compiler_params=pltpu.CompilerParams(vmem_limit_bytes=(14 if shared <= 256 else 52) << 20),
        cost_estimate=pl.CostEstimate(
            flops=8 * leaf_rows * key_rows * span * heads,
            bytes_accessed=4 * leaf_rows * span * heads,
            transcendentals=leaf_rows * key_rows * heads,
        ),
    )(where, mid_len, leaf_len, *own[0], *own[1], *blocks, *roots)
    return out[0], out[1], out[2], out[3 : 3 + slots], out[3 + slots :]


def query_grads(after_this, first, count, so_far, queries, keys, ds):
    rows, cols = queries.shape
    heads = keys.shape[0]
    heads_per = cols // (heads * HD)
    return pl.pallas_call(
        functools.partial(run_query_grads, heads_per, first, count, rows // 2),
        in_specs=[ANY] + [VMEM] * 2 + [ANY] * len(so_far),
        out_specs=ANY,
        out_shape=jax.ShapeDtypeStruct(queries.shape, jnp.bfloat16),
        input_output_aliases={3 + i: i for i in range(len(so_far))},
        scratch_shapes=[
            pltpu.VMEM((rows, count * heads_per * HD), jnp.bfloat16),
            pltpu.SemaphoreType.DMA((count,)),
        ],
        compiler_params=pltpu.CompilerParams(
            vmem_limit_bytes=(10 if keys.shape[1] <= 512 else 32) << 20
        ),
        cost_estimate=cost(1, keys.shape[1] * count // heads, queries, 2 * queries.size),
    )(after_this, keys, ds, *so_far)


def last_grads_kernel(heads_per, first, count, half, after_ref, keys_ref, ds_ref, q0, g0, q1, g1, p_ref, *refs):
    dq_hbm, dk_hbm, dv_hbm, dq_ref, dk_ref, dv_ref, dq_sems, own_sems = refs[1:]
    wait = query_grads_kernel(
        heads_per, first, count, half, False, after_ref, keys_ref, ds_ref, dq_hbm, dq_ref, dq_sems
    )
    own_grads_kernel(after_ref, q0, g0, q1, g1, p_ref, ds_ref, dk_hbm, dv_hbm, dk_ref, dv_ref, own_sems)
    wait()


def last_grads(after_this, first, so_far, leaf_keys, own, keys, p, ds):
    rows, cols = so_far.shape
    heads = keys.shape[0]
    count = heads - first
    span = cols // heads
    own_shape = jax.ShapeDtypeStruct(leaf_keys.shape, jnp.bfloat16)
    return pl.pallas_call(
        functools.partial(last_grads_kernel, span // HD, first, count, rows // 2),
        in_specs=[ANY] + [VMEM] * 7 + [ANY],
        out_specs=[ANY] * 3,
        out_shape=[jax.ShapeDtypeStruct(so_far.shape, jnp.bfloat16), own_shape, own_shape],
        input_output_aliases={8: 0},
        scratch_shapes=[pltpu.VMEM((rows, count * span), jnp.bfloat16)]
        + [pltpu.VMEM(own_shape.shape, jnp.bfloat16)] * 2
        + [pltpu.SemaphoreType.DMA(s) for s in ((count,), (heads, 2))],
        compiler_params=pltpu.CompilerParams(
            vmem_limit_bytes=(10 if ds.shape[1] <= 1024 else 52) << 20
        ),
        cost_estimate=cost(2, keys.shape[1], so_far, 2 * so_far.size),
    )(after_this, keys, ds, *own[0][:2], *own[1][:2], p, so_far)


def gather_kernel(mk_ref, mv_ref, rk_ref, rv_ref, mid_ref, pair_ref):
    mid_ref[...] = jnp.concatenate([mk_ref[...], mv_ref[...]], 0)
    pair_ref[...] = jnp.concatenate([rk_ref[...], rv_ref[...]], 0)


def gather_own(mid_keys, mid_values, root_keys, root_values):
    return pl.pallas_call(
        gather_kernel,
        out_shape=[
            jax.ShapeDtypeStruct((2 * x.shape[0], x.shape[1]), x.dtype)
            for x in (mid_keys, root_keys)
        ],
        compiler_params=pltpu.CompilerParams(vmem_limit_bytes=4 << 20),
    )(*in_hbm(mid_keys, mid_values, root_keys, root_values))


def pack_kernel(root_own, where_ref, mid_len_ref, leaf_len_ref, mid_ref, *refs):
    pairs = [r[...].astype(jnp.float32) for r in refs[:-1]]
    roots = [p[:root_own] for p in pairs] + [p[root_own:] for p in pairs]
    refs[-1][...] = jnp.concatenate(
        [mid_ref[...], jnp.concatenate(roots, 0).astype(jnp.bfloat16)], 0
    )


def pack(scalars, mid, pairs):
    rows = mid.shape[0] + len(pairs) * pairs[0].shape[0]
    return pl.pallas_call(
        functools.partial(pack_kernel, pairs[0].shape[0] // 2),
        in_specs=[SMEM] * 3 + [VMEM] * (1 + len(pairs)),
        out_shape=jax.ShapeDtypeStruct((rows, mid.shape[1]), jnp.bfloat16),
        compiler_params=pltpu.CompilerParams(vmem_limit_bytes=4 << 20),
    )(*scalars, mid, *pairs)


def join_kernel(mid_rows, _, a_ref, b_ref, out_ref):
    rows = a_ref.shape[0]
    out_ref[:mid_rows] = a_ref[:mid_rows]
    out_ref[mid_rows : 2 * mid_rows] = b_ref[:mid_rows]
    roots = [r[mid_rows:rows].astype(jnp.float32) for r in (a_ref, b_ref)]
    out_ref[2 * mid_rows :] = jnp.concatenate(roots, 0).astype(jnp.bfloat16)


def join(first, a, b, mid_rows):
    return pl.pallas_call(
        functools.partial(join_kernel, mid_rows),
        out_shape=jax.ShapeDtypeStruct((2 * a.shape[0], a.shape[1]), a.dtype),
        compiler_params=pltpu.CompilerParams(vmem_limit_bytes=4 << 20),
    )(first, a, b)


def root_of(ref, mid_rows, place):
    if place is None:
        return ref[mid_rows:].astype(jnp.float32)
    both = ref[2 * mid_rows :].astype(jnp.float32)
    rows = both.shape[0] // 2
    return both[place * rows : (place + 1) * rows]


def collect_kernel(slots, mid_rows, _, *refs):
    out_ref = refs[-1]
    roots = [root_of(refs[i], mid_rows, j) for i, j in places(slots)]
    half = roots[0].shape[0] // 2
    out_ref[...] = jnp.concatenate(
        [r[:half] for r in roots] + [r[half:] for r in roots], 0
    ).astype(jnp.bfloat16)


def collect(first, blocks, slots, mid_rows):
    rows = slots * (blocks[0].shape[0] - mid_rows)
    return pl.pallas_call(
        functools.partial(collect_kernel, slots, mid_rows),
        in_specs=[ANY] + [VMEM] * len(blocks),
        out_shape=jax.ShapeDtypeStruct((rows, blocks[0].shape[1]), jnp.bfloat16),
        compiler_params=pltpu.CompilerParams(vmem_limit_bytes=8 << 20),
    )(first, *blocks)


def spread_kernel(slots, mid_rows, _, a_ref, b_ref, *refs):
    mids, outs = refs[:slots], refs[slots:]
    total = a_ref[...].astype(jnp.float32) + b_ref[...].astype(jnp.float32)
    half = total.shape[0] // 2
    part = half // slots
    roots = [
        jnp.concatenate([total[at + s * part : at + (s + 1) * part] for at in (0, half)], 0)
        for s in range(slots)
    ]
    held = {}
    for s, (i, j) in enumerate(places(slots, False)):
        at = mid_rows * (j or 0)
        outs[i][at : at + mid_rows] = mids[s][...]
        held.setdefault(i, []).append(roots[s])
    for i, x in held.items():
        outs[i][len(x) * mid_rows :] = jnp.concatenate(x, 0).astype(jnp.bfloat16)


def spread(first, a, b, mids):
    slots = len(mids)
    mid_rows, cols = mids[0].shape
    rows = mid_rows + a.shape[0] // slots
    found = places(slots, False)
    paired = {i for i, j in found if j is not None}
    shapes = [(2 * rows if i in paired else rows, cols) for i in range(found[-1][0] + 1)]
    return pl.pallas_call(
        functools.partial(spread_kernel, slots, mid_rows),
        in_specs=[ANY] + [VMEM] * (2 + slots),
        out_shape=[jax.ShapeDtypeStruct(x, jnp.bfloat16) for x in shapes],
        compiler_params=pltpu.CompilerParams(vmem_limit_bytes=8 << 20),
    )(*in_hbm(first), a, b, *mids)


def near_sum_kernel(mid_rows, _, a_ref, pair_ref, out_ref):
    pair = pair_ref[mid_rows : 2 * mid_rows].astype(jnp.float32)
    out_ref[:mid_rows] = (a_ref[:mid_rows].astype(jnp.float32) + pair).astype(jnp.bfloat16)
    root = root_of(a_ref, mid_rows, None) + root_of(pair_ref, mid_rows, 1)
    out_ref[mid_rows:] = root.astype(jnp.bfloat16)


def near_sum(first, a, pair, mid_rows):
    return pl.pallas_call(
        functools.partial(near_sum_kernel, mid_rows),
        in_specs=[ANY] + [VMEM] * 2,
        out_shape=jax.ShapeDtypeStruct(a.shape, a.dtype),
        compiler_params=pltpu.CompilerParams(vmem_limit_bytes=4 << 20),
    )(first, a, pair)


def far_sum_kernel(_, a_ref, b_ref, out_ref):
    out_ref[...] = (a_ref[...].astype(jnp.float32) + b_ref[...].astype(jnp.float32)).astype(jnp.bfloat16)


def far_sum(first, a, b):
    return pl.pallas_call(
        far_sum_kernel,
        in_specs=[ANY] + [VMEM] * 2,
        out_shape=jax.ShapeDtypeStruct(a.shape, a.dtype),
        compiler_params=pltpu.CompilerParams(vmem_limit_bytes=4 << 20),
    )(first, a, b)


def mid_sums_kernel(mid_part, *refs):
    for i, o in enumerate(refs[-2:]):
        rows = slice(i * mid_part, (i + 1) * mid_part)
        total = refs[0][rows].astype(jnp.float32)
        for r in refs[1:-2]:
            total = total + r[rows].astype(jnp.float32)
        o[...] = total


def mid_sums(blocks, mid_part):
    return pl.pallas_call(
        functools.partial(mid_sums_kernel, mid_part),
        out_shape=[jax.ShapeDtypeStruct((mid_part, blocks[0].shape[1]), jnp.float32)] * 2,
        compiler_params=pltpu.CompilerParams(vmem_limit_bytes=8 << 20),
    )(*blocks)


def root_sums_kernel(count, mid_rows, root_own, paired, _, *refs):
    root = None
    for i, r in enumerate(refs[:count]):
        x = root_of(r, mid_rows, 0 if paired and i == 1 else None)
        root = x if root is None else root + x
    half = root.shape[0] // 2
    for t, o in enumerate(refs[count:]):
        o[:root_own] = root[t * root_own : (t + 1) * root_own]
        o[root_own:] = root[half + t * root_own : half + (t + 1) * root_own]


def root_sums(first, blocks, mid_rows, root_own, pieces):
    shape = jax.ShapeDtypeStruct((2 * root_own, blocks[0].shape[1]), jnp.float32)
    paired = blocks[1].shape[0] > blocks[0].shape[0]
    return pl.pallas_call(
        functools.partial(root_sums_kernel, len(blocks), mid_rows, root_own, paired),
        in_specs=[ANY] + [VMEM] * len(blocks),
        out_shape=[shape] * pieces,
        compiler_params=pltpu.CompilerParams(vmem_limit_bytes=8 << 20),
    )(*in_hbm(first), *blocks)


def root_kernel(root_own, *refs):
    total = refs[0][...]
    for r in refs[1:-2]:
        total = total + r[...]
    refs[-2][...] = total[:root_own]
    refs[-1][...] = total[root_own:]


def add_roots(pieces):
    rows, cols = pieces[0].shape
    return pl.pallas_call(
        functools.partial(root_kernel, rows // 2),
        out_shape=[jax.ShapeDtypeStruct((rows // 2, cols), jnp.float32)] * 2,
        compiler_params=pltpu.CompilerParams(vmem_limit_bytes=4 << 20),
    )(*pieces)


def swap(x, axis, size, offset):
    return lax.ppermute(x, axis, [(i, i ^ offset) for i in range(size)])


def on_device(
    mids,
    leaves,
    queries,
    out_grad,
    leaf_keys,
    leaf_values,
    mid_keys,
    mid_values,
    root_keys,
    root_values,
    mid_len,
    leaf_len,
):
    mid_part = mid_keys.shape[0]
    root_own = root_keys.shape[0]
    where = lax.axis_index("leaf").reshape(1).astype(jnp.int32)
    mid, pair = gather_own(mid_keys, mid_values, root_keys, root_values)
    mid_rows = 2 * mid_part
    same_core = range(2, mids, 2)
    pairs = [pair] + [swap(pair, "mid", mids, t) for t in same_core]
    block = pack((where, mid_len, leaf_len), mid, pairs)

    def leaf_swap(x, s):
        return swap(x, "leaf", leaves, s)

    far = [s for f in range(4, leaves, 4) for s in (f + 2, f)]
    far_blocks = {s: leaf_swap(block, s) for s in far}
    beside = leaf_swap(block, 1)
    operands = (queries, out_grad, leaf_keys, leaf_values)
    own = [own_part(0, block, *operands)]
    token = own[0][-1]
    blocks = [block, beside]
    if leaves >= 4:
        blocks.append(leaf_swap(join(token, block, beside, mid_rows), 2))
    for f in range(4, leaves, 4):
        x, y = far_blocks[f], far_blocks[f + 2]
        both = join(token, x, y, mid_rows)
        token = both
        blocks += [x, y, leaf_swap(both, 1)]
    own.append(own_part(1, token, *operands))
    root = collect(own[1][-1], blocks, leaves, mid_rows)
    roots = [root, swap(root, "mid", mids, 1)]
    keys, ds, own_p, mid_terms, root_terms = terms_part(
        where, mid_len, leaf_len, leaves, own, blocks, roots, mid_part
    )

    heads = leaf_keys.shape[1] // HD
    cuts = [0, heads // 4, heads * 5 // 8, heads]

    def query_part(first, i, so_far):
        return query_grads(first, cuts[i], cuts[i + 1] - cuts[i], so_far, queries, keys, ds)

    query_grad = query_part(where, 0, ())
    terms = spread(query_grad, root_terms[0], swap(root_terms[1], "mid", mids, 1), mid_terms)
    through = [leaf_swap(terms[s], 1) for s in far]
    query_grad = query_part(terms[0], 1, (query_grad,))
    (token,) = in_hbm(query_grad)
    near = leaf_swap(terms[2], 2) if leaves >= 4 else None
    arrived = [terms[0]] if near is None else [terms[0], near]
    last = terms[0]
    for s, x in zip(far, through):
        last = far_sum(token, terms[s - 1], x)
        token = last
        arrived.append(leaf_swap(last, s))
    beside = terms[1] if near is None else near_sum(last, terms[1], near, mid_rows)
    arrived.append(leaf_swap(beside, 1))
    query_grad, leaf_key_grad, leaf_value_grad = last_grads(
        beside, cuts[2], query_grad, leaf_keys, own, keys, own_p, ds
    )
    pieces = root_sums(leaf_value_grad, arrived, mid_rows, root_own, mids // 2)
    mid_key_grad, mid_value_grad = mid_sums(arrived, mid_part)
    pieces = [pieces[0]] + [swap(x, "mid", mids, t) for t, x in zip(same_core, pieces[1:])]
    root_key_grad, root_value_grad = add_roots(pieces)
    return (
        query_grad,
        leaf_key_grad,
        leaf_value_grad,
        mid_key_grad,
        mid_value_grad,
        root_key_grad,
        root_value_grad,
    )


def solution(mesh):
    both = P(("mid", "leaf"), None)
    in_specs = (both,) * 8 + (P("mid"), P(("mid", "leaf")))
    return jax.shard_map(
        functools.partial(on_device, mesh.shape["mid"], mesh.shape["leaf"]),
        mesh=mesh,
        in_specs=in_specs,
        out_specs=(both,) * 7,
        check_vma=False,
    )
```
